512 devices in a mesh: dp: 16 (over z, core), mp: 32 (over x, y).
Axes of the slice: x: 4, y: 8, z: 8, core: 2. Of those that a mesh axis runs over, the one named last changes fastest.
Arguments:
- tokens: bfloat16 [4096, 2560], P('dp', 'mp'), may hold values from -6 to 6
- cotangent: bfloat16 [4096, 2560], P('dp', 'mp'), may hold values from -6 to 6
- in_blocks: bfloat16 [1024, 128, 128], P('mp'), may hold values from -0.25 to 0.25
- in_lists: int32 [1024, 2], P('mp'), may hold values from -1 to 19, as said below
- out_blocks: bfloat16 [1024, 128, 128], P('mp'), may hold values from -0.1875 to 0.1875
- out_lists: int32 [1024, 2], P('mp'), may hold values from -1 to 19, as said below
Outputs:
- layer_output: bfloat16 [4096, 2560], P('dp', 'mp')
- token_grad: bfloat16 [4096, 2560], P('dp', 'mp')
- in_grad: bfloat16 [1024, 128, 128], P('mp', 'dp')
- out_grad: bfloat16 [1024, 128, 128], P('mp', 'dp')
The draws below stay inside these ranges and needn't reach their ends.
Inputs may be any that keep to these rules, and one draw needn't show every extreme that they name: `in_lists`: each owner's 32 slots list distinct blocks of its 5 block rows (row within the owner, column) in ascending order first, then (-1, -1); in each projection some owner fills all 32 slots. `out_lists`: as for in_lists, drawn independently.
All inputs are finite; a program needn't handle non-finite values.
Results may differ from the reference program's by a relative error of at most 0.023.
Values may be sent and summed in bfloat16 or wider, within the bound.
No kernel may reach another device: no remote copies, remote signals or barrier semaphores. Data moves between devices by JAX's collectives and lax.ppermute only.
A program may use at most 64 MiB of HBM per device.

```python
import math
import jax
import jax.numpy as jnp
from jax import lax

D = 2560
BLK = 128
TOK_GRP = 256
DB = 20
RPO = 5
CAP = 32
SLOTS = 1024
TOKENS = 4096
N_DP = 16
N_MP = 32


def block_lists(key):
    owners = SLOTS // CAP
    places = RPO * DB
    key_count, key_full, key_perm = jax.random.split(key, 3)
    counts = jax.random.randint(key_count, (owners,), CAP * 5 // 16, CAP * 27 // 32)
    full_owner = jax.random.randint(key_full, (), 0, owners)
    counts = jnp.where(jnp.arange(owners) == full_owner, CAP, counts)
    perms = jax.vmap(lambda sub_key: jax.random.permutation(sub_key, places))(jax.random.split(key_perm, owners))
    picked = perms[:, :CAP]
    slot_ids = jnp.arange(CAP)[None, :]
    picked = jnp.where(slot_ids < counts[:, None], picked, places)
    picked = jnp.sort(picked, axis=1)
    live_slot = picked < places
    row_ids = jnp.where(live_slot, picked // DB, -1)
    col_ids = jnp.where(live_slot, picked % DB, -1)
    return jnp.stack([row_ids, col_ids], axis=-1).reshape(SLOTS, 2).astype(jnp.int32)


def draw_in_lists(key, part):
    key = jax.random.fold_in(key, 11)
    return block_lists(key)


def draw_out_lists(key, part):
    key = jax.random.fold_in(key, 23)
    return block_lists(key)


def levels(rng, shape, shards, least, high):
    level = 1.0
    for dim, shards_of in shards:
        steps = jax.random.uniform(jax.random.fold_in(jax.random.fold_in(rng, 6), dim), (shards_of,), jnp.float32, least / len(shards), high / len(shards))
        level = level * jnp.repeat(jnp.exp(steps), shape[dim] // shards_of).reshape((-1,) + (1,) * (len(shape) - 1 - dim))
    return level


def centred(own_key, shape, width, bound, shards=(), kind=jnp.bfloat16):
    result = width * jax.random.normal(own_key, shape, jnp.float32)
    if shards:
        result = result * levels(own_key, shape, shards, -0.22, 0.18)
    return jnp.clip(result, -bound, bound).astype(kind)


def setup_inputs(seed: int = 0) -> dict:
    streams_of = jax.random.split(jax.random.key(seed), 7)
    return {
        "tokens": centred(streams_of[0], (TOKENS, D), 1.0, 6.0, ((0, 16), (1, 32))),
        "cotangent": centred(streams_of[1], (TOKENS, D), 1.0, 6.0, ((0, 16), (1, 32))),
        "in_blocks": centred(streams_of[2], (SLOTS, BLK, BLK), (4 * BLK) ** -0.5, 0.25, ((0, 32),)),
        "in_lists": draw_in_lists(jax.random.fold_in(streams_of[6], 71), 0),
        "out_blocks": centred(streams_of[4], (SLOTS, BLK, BLK), (8 * BLK) ** -0.5, 0.1875, ((0, 32),)),
        "out_lists": draw_out_lists(jax.random.fold_in(streams_of[6], 71), 0),
    }


root_coeff = math.sqrt(2.0 / math.pi)
cubic_coeff = 0.044715

def gelu_pair(pre_values):
    tanh_val = jnp.tanh(root_coeff * (pre_values + cubic_coeff * pre_values * pre_values * pre_values))
    values = 0.5 * pre_values * (1.0 + tanh_val)
    slopes = 0.5 * (1.0 + tanh_val) + 0.5 * pre_values * (1.0 - tanh_val * tanh_val) * root_coeff * (1.0 + 3.0 * cubic_coeff * pre_values * pre_values)
    return (values, slopes)

def tables(lists, row_count, col_count):
    row_ids = lists[:, 0]
    col_ids = lists[:, 1]
    live_mask = (row_ids >= 0).astype(jnp.float32)
    row_hot = (row_ids[:, None] == jnp.arange(row_count, dtype=jnp.int32)[None, :]).astype(jnp.float32)
    col_hot = (col_ids[:, None] == jnp.arange(col_count, dtype=jnp.int32)[None, :]).astype(jnp.float32)
    return (jnp.maximum(row_ids, 0), jnp.maximum(col_ids, 0), live_mask, row_hot, col_hot)

def round_trip(values):
    return lax.optimization_barrier(values.astype(jnp.bfloat16)).astype(jnp.float32)

def reference(tokens, cotangent, in_blocks, in_lists, out_blocks, out_lists):
    highest = lax.Precision.HIGHEST
    col_count = D // BLK
    token_blocks = tokens.reshape(TOKENS, col_count, BLK)
    cot_blocks = cotangent.reshape(TOKENS, col_count, BLK)
    grad_scale = TOKENS ** (-0.5)

    def owner_step(carry, pieces):
        out_sum, input_sum = carry
        in_blk, in_lst, out_blk, out_lst = pieces
        in_rows, in_cols, in_live, in_rhot, in_chot = tables(in_lst, RPO, col_count)
        out_rows, out_cols, out_live, out_rhot, out_chot = tables(out_lst, RPO, col_count)
        x_cols = jnp.take(token_blocks, in_cols, axis=1).astype(jnp.float32)
        pre_terms = jnp.einsum('tsk,sjk->tsj', x_cols, in_blk.astype(jnp.float32), precision=highest)
        hidden = jnp.einsum('tsj,sr->trj', pre_terms, in_rhot, precision=highest)
        activation, slopes = gelu_pair(hidden)
        activation = activation.astype(jnp.bfloat16)
        a_rows = jnp.take(activation, out_rows, axis=1).astype(jnp.float32)
        y_terms = jnp.einsum('tsj,sjk->tsk', a_rows, out_blk.astype(jnp.float32), precision=highest)
        y_part = jnp.einsum('tsk,sd->tdk', y_terms, out_chot, precision=highest)
        g_cols = jnp.take(cot_blocks, out_cols, axis=1).astype(jnp.float32)
        back_terms = jnp.einsum('tsk,sjk->tsj', g_cols, out_blk.astype(jnp.float32), precision=highest)
        d_act = jnp.einsum('tsj,sr->trj', back_terms, out_rhot, precision=highest)
        d_hidden = (d_act * slopes).astype(jnp.bfloat16)
        h_rows = jnp.take(d_hidden, in_rows, axis=1).astype(jnp.float32)
        dx_terms = jnp.einsum('tsj,sjk->tsk', h_rows, in_blk.astype(jnp.float32), precision=highest)
        dx_part = jnp.einsum('tsk,sd->tdk', dx_terms, in_chot, precision=highest)
        out_terms = jnp.einsum('gtsj,gtsk->gsjk', a_rows.reshape(N_DP, TOK_GRP, CAP, BLK), g_cols.reshape(N_DP, TOK_GRP, CAP, BLK), precision=highest)
        out_terms = out_terms * out_live[None, :, None, None]
        out_grad = (lax.optimization_barrier(jnp.sum(round_trip(out_terms), axis=0)) * grad_scale).astype(jnp.bfloat16)
        in_terms = jnp.einsum('gtsj,gtsk->gsjk', h_rows.reshape(N_DP, TOK_GRP, CAP, BLK), x_cols.reshape(N_DP, TOK_GRP, CAP, BLK), precision=highest)
        in_terms = in_terms * in_live[None, :, None, None]
        in_grad = (lax.optimization_barrier(jnp.sum(round_trip(in_terms), axis=0)) * grad_scale).astype(jnp.bfloat16)
        return ((out_sum + round_trip(y_part), input_sum + round_trip(dx_part)), (in_grad, out_grad))
    start = jnp.zeros((TOKENS, col_count, BLK), jnp.float32)
    pieces = (in_blocks.reshape(N_MP, CAP, BLK, BLK), in_lists.reshape(N_MP, CAP, 2), out_blocks.reshape(N_MP, CAP, BLK, BLK), out_lists.reshape(N_MP, CAP, 2))
    (out_sum, input_sum), (in_grads, out_grads) = lax.scan(owner_step, (start, start), pieces)
    layer_output = out_sum.reshape(TOKENS, D).astype(jnp.bfloat16)
    token_grad = input_sum.reshape(TOKENS, D).astype(jnp.bfloat16)
    return (layer_output, token_grad, in_grads.reshape(SLOTS, BLK, BLK), out_grads.reshape(SLOTS, BLK, BLK))
```

```python
import functools
import math

import jax
import jax.numpy as jnp
from jax import lax
from jax.experimental import pallas as pl
from jax.experimental.pallas import tpu as pltpu
from jax.sharding import Mesh
from jax.sharding import PartitionSpec as P

Z, C, X, Y = 8, 2, 4, 8
BLK = 128
CAP = 32
ROWS = 5
COLS = 20
T = 256
FEAT = COLS * BLK
OWN = FEAT // (X * Y)
SUB = BLK // (Z * C)

ROOT_COEFF = math.sqrt(2.0 / math.pi)
CUBIC_COEFF = 0.044715


def gelu_pair(pre):
    tanh_val = jnp.tanh(ROOT_COEFF * (pre + CUBIC_COEFF * pre * pre * pre))
    values = 0.5 * pre * (1.0 + tanh_val)
    slopes = 0.5 * (1.0 + tanh_val) + 0.5 * pre * (1.0 - tanh_val * tanh_val) * ROOT_COEFF * (
        1.0 + 3.0 * CUBIC_COEFF * pre * pre
    )
    return values, slopes


def dot(a, b, dims):
    return lax.dot_general(a, b, (dims, ((), ())), preferred_element_type=jnp.float32)


def place(lists, s):
    row, col = lists[2 * s], lists[2 * s + 1]
    live = jnp.where(row >= 0, 1.0, 0.0).astype(jnp.float32)
    row = jnp.maximum(row, 0)
    return row, pl.multiple_of(jnp.maximum(col, 0) * BLK, BLK), live


def units_kernel(core, in_l, out_l, xg, w_in, w_out, keep, send, act, dh, hidden, d_act):
    hidden[...] = jnp.zeros_like(hidden)
    d_act[...] = jnp.zeros_like(d_act)

    def product(s, carry):
        row, col, live = place(in_l, s)
        hidden[row] += dot(w_in[s], xg[pl.ds(col, BLK), :T], ((1,), (0,))) * live
        row, col, live = place(out_l, s)
        d_act[row] += dot(w_out[s], xg[pl.ds(col, BLK), T:], ((1,), (0,))) * live
        return carry

    lax.fori_loop(0, CAP, product, 0, unroll=8)
    for row in range(ROWS):
        values, slopes = gelu_pair(hidden[row])
        act[row] = values.astype(act.dtype)
        dh[row] = (d_act[row] * slopes).astype(dh.dtype)

    first = core[0] == 0
    scale = float(T * Z * C) ** -0.5

    def pair(p, carry):
        for which, (lists, units, lo) in enumerate(((out_l, act, T), (in_l, dh, 0))):
            parts = []
            for i in range(2):
                row, col, live = place(lists, 2 * p + i)
                part = dot(units[row], xg[pl.ds(col, BLK), lo : lo + T], ((1,), (1,)))
                parts.append((part * (live * scale)).reshape(Z, C, SUB, BLK))
            both = jnp.stack(parts, axis=2).reshape(Z, C, 2 * SUB, BLK)
            at = pl.multiple_of((which * CAP + 2 * p) * SUB, 2 * SUB)
            keep[:, pl.ds(at, 2 * SUB), :] = jnp.where(first, both[:, 0], both[:, 1]).astype(
                keep.dtype
            )
            send[:, pl.ds(at, 2 * SUB), :] = jnp.where(first, both[:, 1], both[:, 0]).astype(
                send.dtype
            )
        return carry

    lax.fori_loop(0, CAP // 2, pair, 0, unroll=4)


def partials_kernel(in_l, out_l, act, dh, w_in, w_out, out, total):
    total[...] = jnp.zeros_like(total)

    def product(s, carry):
        row, col, live = place(out_l, s)
        total[pl.ds(col, BLK), :T] += dot(w_out[s], act[row], ((0,), (0,))) * live
        row, col, live = place(in_l, s)
        total[pl.ds(col, BLK), T:] += dot(w_in[s], dh[row], ((0,), (0,))) * live
        return carry

    lax.fori_loop(0, CAP, product, 0, unroll=8)
    out[...] = total[...].astype(out.dtype)


SMEM = pl.BlockSpec(memory_space=pltpu.SMEM)
VMEM = pl.BlockSpec(memory_space=pltpu.VMEM)
LIMIT = pltpu.CompilerParams(vmem_limit_bytes=48 * 1024 * 1024)


def units_call(core, in_l, out_l, xg, w_in, w_out, interpret=False):
    bf = jnp.bfloat16
    half = jax.ShapeDtypeStruct((Z, 2 * CAP * SUB, BLK), bf)
    rows = jax.ShapeDtypeStruct((ROWS, BLK, T), bf)
    return pl.pallas_call(
        units_kernel,
        out_shape=(half, half, rows, rows),
        in_specs=[SMEM] * 3 + [VMEM] * 3,
        out_specs=[VMEM] * 4,
        scratch_shapes=[pltpu.VMEM((ROWS, BLK, T), jnp.float32)] * 2,
        compiler_params=LIMIT,
        interpret=interpret,
    )(core, in_l, out_l, xg, w_in, w_out)


def partials_call(in_l, out_l, act, dh, w_in, w_out, interpret=False):
    return pl.pallas_call(
        partials_kernel,
        out_shape=jax.ShapeDtypeStruct((FEAT, 2 * T), jnp.bfloat16),
        in_specs=[SMEM] * 2 + [VMEM] * 4,
        out_specs=VMEM,
        scratch_shapes=[pltpu.VMEM((FEAT, 2 * T), jnp.float32)],
        compiler_params=LIMIT,
        interpret=interpret,
    )(in_l, out_l, act, dh, w_in, w_out)


def exchange(x, axis):
    return lax.all_to_all(x, axis, split_axis=0, concat_axis=0)


def spread(x, axis, size):
    return exchange(jnp.broadcast_to(x[None], (size,) + x.shape), axis)


def body(tokens, cotangent, in_blocks, in_lists, out_blocks, out_lists):
    bf, f32 = jnp.bfloat16, jnp.float32
    in_l, out_l = in_lists.reshape(-1), out_lists.reshape(-1)
    own = jnp.concatenate([tokens.T, cotangent.T], axis=1)
    along_y = spread(own, "y", Y).reshape(Y * OWN, 2 * T)
    xg = spread(along_y, "x", X).reshape(FEAT, 2 * T)
    core = lax.axis_index("c").astype(jnp.int32).reshape(1)
    keep, send, act, dh = units_call(core, in_l, out_l, xg, in_blocks, out_blocks)
    got = lax.ppermute(send, "c", [(0, 1), (1, 0)])
    parts = partials_call(in_l, out_l, act, dh, in_blocks, out_blocks)
    grads = (keep.astype(f32) + got.astype(f32)).astype(bf)
    grads, parts = lax.optimization_barrier((grads, parts))
    grads = lax.psum_scatter(grads, "z", scatter_dimension=0)
    parts = exchange(parts.reshape(X, Y * OWN, 2 * T), "x")
    parts = jnp.sum(parts.astype(f32), axis=0).astype(bf)
    parts = exchange(parts.reshape(Y, OWN, 2 * T), "y")
    sums = jnp.sum(parts.astype(f32), axis=0).astype(bf)
    grads = grads.reshape(2, CAP, SUB, BLK)
    return sums[:, :T].T, sums[:, T:].T, grads[1], grads[0]


def solution(mesh):
    fine = Mesh(mesh.devices.reshape(Z, C, X, Y), ("z", "c", "x", "y"))
    dp, mp = ("z", "c"), ("x", "y")
    blocks, lists = P(mp, None, None), P(mp, None)
    return jax.shard_map(
        body,
        mesh=fine,
        in_specs=(P(dp, mp), P(dp, mp), blocks, lists, blocks, lists),
        out_specs=(P(dp, mp), P(dp, mp), P(mp, dp, None), P(mp, dp, None)),
        check_vma=False,
    )
```

```python
import functools
import math

import jax
import jax.numpy as jnp
from jax import lax
from jax.experimental import pallas as pl
from jax.experimental.pallas import tpu as pltpu
from jax.sharding import Mesh
from jax.sharding import PartitionSpec as P

Z, C, X, Y = 8, 2, 4, 8
BLK = 128
CAP = 32
ROWS = 5
COLS = 20
T = 256
FEAT = COLS * BLK
OWN = FEAT // (X * Y)
SUB = BLK // (Z * C)

ROOT_COEFF = math.sqrt(2.0 / math.pi)
CUBIC_COEFF = 0.044715


def gelu_pair(pre):
    tanh_val = jnp.tanh(ROOT_COEFF * (pre + CUBIC_COEFF * pre * pre * pre))
    values = 0.5 * pre * (1.0 + tanh_val)
    slopes = 0.5 * (1.0 + tanh_val) + 0.5 * pre * (1.0 - tanh_val * tanh_val) * ROOT_COEFF * (
        1.0 + 3.0 * CUBIC_COEFF * pre * pre
    )
    return values, slopes


def dot(a, b, dims):
    return lax.dot_general(a, b, (dims, ((), ())), preferred_element_type=jnp.float32)


def place(lists, s):
    row, col = lists[2 * s], lists[2 * s + 1]
    live = jnp.where(row >= 0, 1.0, 0.0).astype(jnp.float32)
    row = jnp.maximum(row, 0)
    return row, pl.multiple_of(jnp.maximum(col, 0) * BLK, BLK), live


def forward_kernel(in_l, out_l, x, w_in, w_out, act, slope, part, hidden, total):
    hidden[...] = jnp.zeros_like(hidden)
    total[...] = jnp.zeros_like(total)

    def up(s, carry):
        row, col, live = place(in_l, s)
        hidden[row] += dot(w_in[s], x[pl.ds(col, BLK), :], ((1,), (0,))) * live
        return carry

    def down(s, carry):
        row, col, live = place(out_l, s)
        total[pl.ds(col, BLK), :] += dot(w_out[s], act[row], ((0,), (0,))) * live
        return carry

    lax.fori_loop(0, CAP, up, 0, unroll=8)
    for row in range(ROWS):
        values, slopes = gelu_pair(hidden[row])
        act[row] = values.astype(act.dtype)
        slope[row] = slopes
    lax.fori_loop(0, CAP, down, 0, unroll=8)
    part[...] = total[...].astype(part.dtype)


def backward_kernel(in_l, out_l, g, slope, w_in, w_out, dh, part, d_act, total):
    d_act[...] = jnp.zeros_like(d_act)
    total[...] = jnp.zeros_like(total)

    def up(s, carry):
        row, col, live = place(out_l, s)
        d_act[row] += dot(w_out[s], g[pl.ds(col, BLK), :], ((1,), (0,))) * live
        return carry

    def down(s, carry):
        row, col, live = place(in_l, s)
        total[pl.ds(col, BLK), :] += dot(w_in[s], dh[row], ((0,), (0,))) * live
        return carry

    lax.fori_loop(0, CAP, up, 0, unroll=8)
    for row in range(ROWS):
        dh[row] = (d_act[row] * slope[row]).astype(dh.dtype)
    lax.fori_loop(0, CAP, down, 0, unroll=8)
    part[...] = total[...].astype(part.dtype)


def grads_kernel(core, in_l, out_l, x, g, act, dh, keep, send):
    first = core[0] == 0
    scale = float(T * Z * C) ** -0.5

    def pair(p, carry):
        for which, (lists, units, wide) in enumerate(((out_l, act, g), (in_l, dh, x))):
            parts = []
            for i in range(2):
                row, col, live = place(lists, 2 * p + i)
                part = dot(units[row], wide[pl.ds(col, BLK), :], ((1,), (1,)))
                parts.append((part * (live * scale)).reshape(Z, C, SUB, BLK))
            both = jnp.stack(parts, axis=2).reshape(Z, C, 2 * SUB, BLK)
            at = pl.multiple_of((which * CAP + 2 * p) * SUB, 2 * SUB)
            keep[:, pl.ds(at, 2 * SUB), :] = jnp.where(first, both[:, 0], both[:, 1]).astype(
                keep.dtype
            )
            send[:, pl.ds(at, 2 * SUB), :] = jnp.where(first, both[:, 1], both[:, 0]).astype(
                send.dtype
            )
        return carry

    lax.fori_loop(0, CAP // 2, pair, 0, unroll=4)


SMEM = pl.BlockSpec(memory_space=pltpu.SMEM)
VMEM = pl.BlockSpec(memory_space=pltpu.VMEM)
LIMIT = pltpu.CompilerParams(vmem_limit_bytes=48 * 1024 * 1024)
UNITS = (ROWS, BLK, T)
INTERPRET = False


def shape(dims, dtype=jnp.bfloat16):
    return jax.ShapeDtypeStruct(dims, dtype)


def call(kernel, outs, scalars, arrays, scratch=()):
    return pl.pallas_call(
        kernel,
        out_shape=outs,
        in_specs=[SMEM] * len(scalars) + [VMEM] * len(arrays),
        out_specs=[VMEM] * len(outs),
        scratch_shapes=[pltpu.VMEM(dims, jnp.float32) for dims in scratch],
        compiler_params=LIMIT,
        interpret=INTERPRET,
    )(*scalars, *arrays)


def forward(in_l, out_l, x, w_in, w_out):
    outs = (shape(UNITS), shape(UNITS, jnp.float32), shape((FEAT, T)))
    return call(forward_kernel, outs, (in_l, out_l), (x, w_in, w_out), (UNITS, (FEAT, T)))


def backward(in_l, out_l, g, slope, w_in, w_out):
    outs = (shape(UNITS), shape((FEAT, T)))
    return call(backward_kernel, outs, (in_l, out_l), (g, slope, w_in, w_out), (UNITS, (FEAT, T)))


def block_grads(core, in_l, out_l, x, g, act, dh):
    half = shape((Z, 2 * CAP * SUB, BLK))
    return call(grads_kernel, (half, half), (core, in_l, out_l), (x, g, act, dh))


def exchange(x, axis):
    return lax.all_to_all(x, axis, split_axis=0, concat_axis=0)


def spread(x, axis, size):
    return exchange(jnp.broadcast_to(x[None], (size,) + x.shape), axis)


def added(parts):
    return jnp.sum(parts.astype(jnp.float32), axis=0).astype(parts.dtype)


def body(tokens, cotangent, in_blocks, in_lists, out_blocks, out_lists):
    bf, f32 = jnp.bfloat16, jnp.float32
    in_l, out_l = in_lists.reshape(-1), out_lists.reshape(-1)
    core = lax.axis_index("c").astype(jnp.int32).reshape(1)
    x = spread(tokens.T, "y", Y).reshape(Y * OWN, T)
    g = spread(cotangent.T, ("x", "y"), X * Y).reshape(FEAT, T)
    x = spread(x, "x", X).reshape(FEAT, T)
    act, slope, y_part = forward(in_l, out_l, x, in_blocks, out_blocks)
    y_part = exchange(y_part.reshape(X, Y * OWN, T), "x")
    dh, dx_part = backward(in_l, out_l, g, slope, in_blocks, out_blocks)
    dx_part = exchange(dx_part.reshape(X * Y, OWN, T), ("x", "y"))
    keep, send = block_grads(core, in_l, out_l, x, g, act, dh)
    got = lax.ppermute(send, "c", [(0, 1), (1, 0)])
    grads = exchange((keep.astype(f32) + got.astype(f32)).astype(bf), "z")
    y_part = exchange(added(y_part).reshape(Y, OWN, T), "y")
    grads = added(grads).reshape(2, CAP, SUB, BLK)
    return added(y_part).T, added(dx_part).T, grads[1], grads[0]


def solution(mesh):
    fine = Mesh(mesh.devices.reshape(Z, C, X, Y), ("z", "c", "x", "y"))
    dp, mp = ("z", "c"), ("x", "y")
    blocks, lists = P(mp, None, None), P(mp, None)
    return jax.shard_map(
        body,
        mesh=fine,
        in_specs=(P(dp, mp), P(dp, mp), blocks, lists, blocks, lists),
        out_specs=(P(dp, mp), P(dp, mp), P(mp, dp, None), P(mp, dp, None)),
        check_vma=False,
    )
```

```python
import functools
import math

import jax
import jax.numpy as jnp
from jax import lax
from jax.experimental import pallas as pl
from jax.experimental.pallas import tpu as pltpu
from jax.sharding import Mesh
from jax.sharding import PartitionSpec as P

Z, C, X, Y = 8, 2, 4, 8
BLK = 128
CAP = 32
ROWS = 5
COLS = 20
T = 256
FEAT = COLS * BLK
OWN = FEAT // (X * Y)
SUB = BLK // (Z * C)

ROOT_COEFF = math.sqrt(2.0 / math.pi)
CUBIC_COEFF = 0.044715


def gelu_pair(pre):
    tanh_val = jnp.tanh(ROOT_COEFF * (pre + CUBIC_COEFF * pre * pre * pre))
    values = 0.5 * pre * (1.0 + tanh_val)
    slopes = 0.5 * (1.0 + tanh_val) + 0.5 * pre * (1.0 - tanh_val * tanh_val) * ROOT_COEFF * (
        1.0 + 3.0 * CUBIC_COEFF * pre * pre
    )
    return values, slopes


def dot(a, b, dims):
    return lax.dot_general(a, b, (dims, ((), ())), preferred_element_type=jnp.float32)


def place(lists, s):
    row, col = lists[2 * s], lists[2 * s + 1]
    live = jnp.where(row >= 0, 1.0, 0.0).astype(jnp.float32)
    row = jnp.maximum(row, 0)
    return row, pl.multiple_of(jnp.maximum(col, 0) * BLK, BLK), live


def units_kernel(at_z, core, in_l, out_l, xg, w_in, w_out, keep, send, act, dh, hidden, d_act):
    hidden[...] = jnp.zeros_like(hidden)
    d_act[...] = jnp.zeros_like(d_act)

    def product(s, carry):
        row, col, live = place(in_l, s)
        hidden[row] += dot(w_in[s], xg[pl.ds(col, BLK), :T], ((1,), (0,))) * live
        row, col, live = place(out_l, s)
        d_act[row] += dot(w_out[s], xg[pl.ds(col, BLK), T:], ((1,), (0,))) * live
        return carry

    lax.fori_loop(0, CAP, product, 0, unroll=8)
    for row in range(ROWS):
        values, slopes = gelu_pair(hidden[row])
        act[row] = values.astype(act.dtype)
        dh[row] = (d_act[row] * slopes).astype(dh.dtype)

    first = core[0] == 0
    scale = float(T * Z * C) ** -0.5

    def pair(p, carry):
        for which, (lists, units, lo) in enumerate(((out_l, act, T), (in_l, dh, 0))):
            parts = []
            for i in range(2):
                row, col, live = place(lists, 2 * p + i)
                part = dot(units[row], xg[pl.ds(col, BLK), lo : lo + T], ((1,), (1,)))
                parts.append((part * (live * scale)).reshape(Z, C, SUB, BLK))
            both = jnp.stack(parts, axis=2).reshape(Z, C, 2 * SUB, BLK)
            at = pl.multiple_of((which * CAP + 2 * p) * SUB, 2 * SUB)
            mine = jnp.where(first, both[:, 0], both[:, 1]).astype(keep.dtype)
            others = jnp.where(first, both[:, 1], both[:, 0]).astype(send.dtype)
            for z in range(Z):
                step = lax.rem(z + Z - at_z[0], Z)
                keep[step, pl.ds(at, 2 * SUB), :] = mine[z]
                send[step, pl.ds(at, 2 * SUB), :] = others[z]
        return carry

    lax.fori_loop(0, CAP // 2, pair, 0, unroll=4)


def partials_kernel(in_l, out_l, act, dh, w_in, w_out, out, total):
    total[...] = jnp.zeros_like(total)

    def product(s, carry):
        row, col, live = place(out_l, s)
        total[pl.ds(col, BLK), :T] += dot(w_out[s], act[row], ((0,), (0,))) * live
        row, col, live = place(in_l, s)
        total[pl.ds(col, BLK), T:] += dot(w_in[s], dh[row], ((0,), (0,))) * live
        return carry

    lax.fori_loop(0, CAP, product, 0, unroll=8)
    out[...] = total[...].astype(out.dtype)


def pair_kernel(keep, got, *outs):
    for step, out in enumerate(outs):
        both = keep[step].astype(jnp.float32) + got[step].astype(jnp.float32)
        out[...] = both.astype(out.dtype)


SMEM = pl.BlockSpec(memory_space=pltpu.SMEM)
VMEM = pl.BlockSpec(memory_space=pltpu.VMEM)
LIMIT = pltpu.CompilerParams(vmem_limit_bytes=48 * 1024 * 1024)


def units_call(at_z, core, in_l, out_l, xg, w_in, w_out, interpret=False):
    bf = jnp.bfloat16
    half = jax.ShapeDtypeStruct((Z, 2 * CAP * SUB, BLK), bf)
    rows = jax.ShapeDtypeStruct((ROWS, BLK, T), bf)
    return pl.pallas_call(
        units_kernel,
        out_shape=(half, half, rows, rows),
        in_specs=[SMEM] * 4 + [VMEM] * 3,
        out_specs=[VMEM] * 4,
        scratch_shapes=[pltpu.VMEM((ROWS, BLK, T), jnp.float32)] * 2,
        compiler_params=LIMIT,
        interpret=interpret,
    )(at_z, core, in_l, out_l, xg, w_in, w_out)


def partials_call(in_l, out_l, act, dh, w_in, w_out, interpret=False):
    return pl.pallas_call(
        partials_kernel,
        out_shape=jax.ShapeDtypeStruct((FEAT, 2 * T), jnp.bfloat16),
        in_specs=[SMEM] * 2 + [VMEM] * 4,
        out_specs=VMEM,
        scratch_shapes=[pltpu.VMEM((FEAT, 2 * T), jnp.float32)],
        compiler_params=LIMIT,
        interpret=interpret,
    )(in_l, out_l, act, dh, w_in, w_out)


def pair_call(keep, got):
    out = jax.ShapeDtypeStruct(keep.shape[1:], keep.dtype)
    return pl.pallas_call(
        pair_kernel,
        out_shape=(out,) * Z,
        in_specs=[VMEM] * 2,
        out_specs=[VMEM] * Z,
        compiler_params=LIMIT,
    )(keep, got)


def exchange(x, axis):
    return lax.all_to_all(x, axis, split_axis=0, concat_axis=0)


def spread(x, axis, size):
    return exchange(jnp.broadcast_to(x[None], (size,) + x.shape), axis)


def body(tokens, cotangent, in_blocks, in_lists, out_blocks, out_lists):
    bf, f32 = jnp.bfloat16, jnp.float32
    in_l, out_l = in_lists.reshape(-1), out_lists.reshape(-1)
    own = jnp.concatenate([tokens.T, cotangent.T], axis=1)
    along_y = spread(own, "y", Y).reshape(Y * OWN, 2 * T)
    xg = spread(along_y, "x", X).reshape(FEAT, 2 * T)
    core = lax.axis_index("c").astype(jnp.int32).reshape(1)
    at_z = lax.axis_index("z").astype(jnp.int32).reshape(1)
    keep, send, act, dh = units_call(at_z, core, in_l, out_l, xg, in_blocks, out_blocks)
    got = lax.ppermute(send, "c", [(0, 1), (1, 0)])
    parts = partials_call(in_l, out_l, act, dh, in_blocks, out_blocks)
    steps = pair_call(keep, got)
    steps, parts = lax.optimization_barrier((steps, parts))
    parts = exchange(parts.reshape(X, Y * OWN, 2 * T), "x")

    def along_z(step):
        return lax.ppermute(steps[step], "z", [(z, (z + step) % Z) for z in range(Z)])

    early = [along_z(step) for step in range(2, Z - 1)]
    parts, early = lax.optimization_barrier((parts, early))
    moved = [*early, along_z(1), along_z(Z - 1)]
    parts = jnp.sum(parts.astype(f32), axis=0).astype(bf)
    parts = exchange(parts.reshape(Y, OWN, 2 * T), "y")
    sums = jnp.sum(parts.astype(f32), axis=0).astype(bf)
    grads = sum((m.astype(f32) for m in moved), steps[0].astype(f32))
    grads = grads.astype(bf).reshape(2, CAP, SUB, BLK)
    return sums[:, :T].T, sums[:, T:].T, grads[1], grads[0]


def solution(mesh):
    fine = Mesh(mesh.devices.reshape(Z, C, X, Y), ("z", "c", "x", "y"))
    dp, mp = ("z", "c"), ("x", "y")
    blocks, lists = P(mp, None, None), P(mp, None)
    return jax.shard_map(
        body,
        mesh=fine,
        in_specs=(P(dp, mp), P(dp, mp), blocks, lists, blocks, lists),
        out_specs=(P(dp, mp), P(dp, mp), P(mp, dp, None), P(mp, dp, None)),
        check_vma=False,
    )
```

```python
import functools
import math

import jax
import jax.numpy as jnp
from jax import lax
from jax.experimental import pallas as pl
from jax.experimental.pallas import tpu as pltpu
from jax.sharding import Mesh
from jax.sharding import PartitionSpec as P

Z, C, X, Y = 8, 2, 4, 8
BLK = 128
CAP = 32
ROWS = 5
COLS = 20
T = 256
FEAT = COLS * BLK
OWN = FEAT // (X * Y)
SUB = BLK // (Z * C)

ROOT_COEFF = math.sqrt(2.0 / math.pi)
CUBIC_COEFF = 0.044715


def gelu_pair(pre):
    tanh_val = jnp.tanh(ROOT_COEFF * (pre + CUBIC_COEFF * pre * pre * pre))
    values = 0.5 * pre * (1.0 + tanh_val)
    slopes = 0.5 * (1.0 + tanh_val) + 0.5 * pre * (1.0 - tanh_val * tanh_val) * ROOT_COEFF * (
        1.0 + 3.0 * CUBIC_COEFF * pre * pre
    )
    return values, slopes


def dot(a, b, dims):
    return lax.dot_general(a, b, (dims, ((), ())), preferred_element_type=jnp.float32)


def place(lists, s):
    row, col = lists[2 * s], lists[2 * s + 1]
    live = jnp.where(row >= 0, 1.0, 0.0).astype(jnp.float32)
    row = jnp.maximum(row, 0)
    return row, pl.multiple_of(jnp.maximum(col, 0) * BLK, BLK), live


def slot_of(z, target):
    odd = lax.rem(target + Z - z, 2)
    base = z + odd * (1 - 2 * lax.rem(z, 2))
    return odd * (Z // 2) + lax.rem(target + Z - base, Z) // 2


def units_kernel(at_z, core, in_l, out_l, xg, w_in, w_out, keep, send, act, dh, hidden, d_act):
    hidden[...] = jnp.zeros_like(hidden)
    d_act[...] = jnp.zeros_like(d_act)

    def product(s, carry):
        row, col, live = place(in_l, s)
        hidden[row] += dot(w_in[s], xg[pl.ds(col, BLK), :T], ((1,), (0,))) * live
        row, col, live = place(out_l, s)
        d_act[row] += dot(w_out[s], xg[pl.ds(col, BLK), T:], ((1,), (0,))) * live
        return carry

    lax.fori_loop(0, CAP, product, 0, unroll=8)
    for row in range(ROWS):
        values, slopes = gelu_pair(hidden[row])
        act[row] = values.astype(act.dtype)
        dh[row] = (d_act[row] * slopes).astype(dh.dtype)

    first = core[0] == 0
    scale = float(T * Z * C) ** -0.5
    slots = [slot_of(at_z[0], z) for z in range(Z)]

    def pair(p, carry):
        for which, (lists, units, lo) in enumerate(((out_l, act, T), (in_l, dh, 0))):
            parts = []
            for i in range(2):
                row, col, live = place(lists, 2 * p + i)
                part = dot(units[row], xg[pl.ds(col, BLK), lo : lo + T], ((1,), (1,)))
                parts.append((part * (live * scale)).reshape(Z, C, SUB, BLK))
            both = jnp.stack(parts, axis=2).reshape(Z, C, 2 * SUB, BLK)
            at = pl.multiple_of((which * CAP + 2 * p) * SUB, 2 * SUB)
            mine = jnp.where(first, both[:, 0], both[:, 1]).astype(keep.dtype)
            others = jnp.where(first, both[:, 1], both[:, 0]).astype(send.dtype)
            for z, slot in enumerate(slots):
                keep[slot, pl.ds(at, 2 * SUB), :] = mine[z]
                send[slot, pl.ds(at, 2 * SUB), :] = others[z]
        return carry

    lax.fori_loop(0, CAP // 2, pair, 0, unroll=4)


def partials_kernel(in_l, out_l, act, dh, w_in, w_out, out, total):
    total[...] = jnp.zeros_like(total)

    def product(s, carry):
        row, col, live = place(out_l, s)
        total[pl.ds(col, BLK), :T] += dot(w_out[s], act[row], ((0,), (0,))) * live
        row, col, live = place(in_l, s)
        total[pl.ds(col, BLK), T:] += dot(w_in[s], dh[row], ((0,), (0,))) * live
        return carry

    lax.fori_loop(0, CAP, product, 0, unroll=8)
    out[...] = total[...].astype(out.dtype)


def cores_kernel(keep, got, near, far):
    for slot in range(Z):
        both = keep[slot].astype(jnp.float32) + got[slot].astype(jnp.float32)
        out = near if slot < Z // 2 else far
        out[slot % (Z // 2)] = both.astype(out.dtype)


def pairs_kernel(near, got, *outs):
    for slot, out in enumerate(outs):
        both = near[slot].astype(jnp.float32) + got[slot].astype(jnp.float32)
        out[...] = both.astype(out.dtype)


SMEM = pl.BlockSpec(memory_space=pltpu.SMEM)
VMEM = pl.BlockSpec(memory_space=pltpu.VMEM)
LIMIT = pltpu.CompilerParams(vmem_limit_bytes=24 * 1024 * 1024)


def units_call(at_z, core, in_l, out_l, xg, w_in, w_out, interpret=False):
    bf = jnp.bfloat16
    half = jax.ShapeDtypeStruct((Z, 2 * CAP * SUB, BLK), bf)
    rows = jax.ShapeDtypeStruct((ROWS, BLK, T), bf)
    return pl.pallas_call(
        units_kernel,
        out_shape=(half, half, rows, rows),
        in_specs=[SMEM] * 4 + [VMEM] * 3,
        out_specs=[VMEM] * 4,
        scratch_shapes=[pltpu.VMEM((ROWS, BLK, T), jnp.float32)] * 2,
        compiler_params=LIMIT,
        interpret=interpret,
    )(at_z, core, in_l, out_l, xg, w_in, w_out)


def partials_call(in_l, out_l, act, dh, w_in, w_out, interpret=False):
    return pl.pallas_call(
        partials_kernel,
        out_shape=jax.ShapeDtypeStruct((FEAT, 2 * T), jnp.bfloat16),
        in_specs=[SMEM] * 2 + [VMEM] * 4,
        out_specs=VMEM,
        scratch_shapes=[pltpu.VMEM((FEAT, 2 * T), jnp.float32)],
        compiler_params=LIMIT,
        interpret=interpret,
    )(in_l, out_l, act, dh, w_in, w_out)


def add_call(kernel, one, other, outs):
    return pl.pallas_call(
        kernel,
        out_shape=tuple(jax.ShapeDtypeStruct(dims, one.dtype) for dims in outs),
        in_specs=[VMEM] * 2,
        out_specs=[VMEM] * len(outs),
        compiler_params=LIMIT,
    )(one, other)


def exchange(x, axis):
    return lax.all_to_all(x, axis, split_axis=0, concat_axis=0)


def spread(x, axis, size):
    return exchange(jnp.broadcast_to(x[None], (size,) + x.shape), axis)


def body(tokens, cotangent, in_blocks, in_lists, out_blocks, out_lists):
    bf, f32 = jnp.bfloat16, jnp.float32
    in_l, out_l = in_lists.reshape(-1), out_lists.reshape(-1)
    own = jnp.concatenate([tokens.T, cotangent.T], axis=1)
    core = lax.axis_index("c").astype(jnp.int32).reshape(1)
    at_z = lax.axis_index("z").astype(jnp.int32).reshape(1)
    own, in_l, out_l, core, at_z = lax.optimization_barrier((own, in_l, out_l, core, at_z))
    along_y = spread(own, "y", Y).reshape(Y * OWN, 2 * T)
    xg = spread(along_y, "x", X).reshape(FEAT, 2 * T)
    keep, send, act, dh = units_call(at_z, core, in_l, out_l, xg, in_blocks, out_blocks)
    got = lax.ppermute(send, "c", [(0, 1), (1, 0)])
    parts = partials_call(in_l, out_l, act, dh, in_blocks, out_blocks)
    half = (Z // 2,) + keep.shape[1:]
    near, far = add_call(cores_kernel, keep, got, (half, half))
    near, far, parts = lax.optimization_barrier((near, far, parts))
    parts = exchange(parts.reshape(X, Y * OWN, 2 * T), "x")
    got = lax.ppermute(far, "z", [(z, z ^ 1) for z in range(Z)])
    parts, got = lax.optimization_barrier((parts, got))
    own, *steps = add_call(pairs_kernel, near, got, (half[1:],) * (Z // 2))
    moved = [
        lax.ppermute(step, "z", [(z, (z + 2 * k) % Z) for z in range(Z)])
        for k, step in enumerate(steps, 1)
    ]
    parts = jnp.sum(parts.astype(f32), axis=0).astype(bf)
    parts = exchange(parts.reshape(Y, OWN, 2 * T), "y")
    sums = jnp.sum(parts.astype(f32), axis=0).astype(bf)
    grads = sum((m.astype(f32) for m in moved), own.astype(f32))
    grads = grads.astype(bf).reshape(2, CAP, SUB, BLK)
    return sums[:, :T].T, sums[:, T:].T, grads[1], grads[0]


def solution(mesh):
    fine = Mesh(mesh.devices.reshape(Z, C, X, Y), ("z", "c", "x", "y"))
    dp, mp = ("z", "c"), ("x", "y")
    blocks, lists = P(mp, None, None), P(mp, None)
    return jax.shard_map(
        body,
        mesh=fine,
        in_specs=(P(dp, mp), P(dp, mp), blocks, lists, blocks, lists),
        out_specs=(P(dp, mp), P(dp, mp), P(mp, dp, None), P(mp, dp, None)),
        check_vma=False,
    )
```

```python
import math

import jax
import jax.numpy as jnp
from jax import lax
from jax.experimental import pallas as pl
from jax.experimental.pallas import tpu as pltpu
from jax.sharding import Mesh
from jax.sharding import PartitionSpec as P

Z, C, X, Y = 8, 2, 4, 8
BLK = 128
CAP = 32
ROWS = 5
COLS = 20
T = 256
FEAT = COLS * BLK
OWN = FEAT // (X * Y)
SUB = BLK // (Z * C)
NEAR = 4
FAR = X * Y // NEAR
HALF = Z // 2
UNITS = (ROWS, BLK, T)
STEP = (2 * CAP * SUB, BLK)

ROOT_COEFF = math.sqrt(2.0 / math.pi)
CUBIC_COEFF = 0.044715


def owner_at(core, near, far):
    x = lax.rem(2 * (far // (Y // 2)) + near // 2 + core, X)
    y = lax.rem(2 * (far % (Y // 2)) + near % 2 + core, Y)
    return x * Y + y


def device_at(core, near, far):
    x = (2 * (far // (Y // 2)) + near // 2 + core) % X
    y = (2 * (far % (Y // 2)) + near % 2 + core) % Y
    return (core * X + x) * Y + y


NEAR_GROUPS = [[device_at(c, n, f) for n in range(NEAR)] for c in range(C) for f in range(FAR)]
FAR_GROUPS = [[device_at(c, n, f) for f in range(FAR)] for c in range(C) for n in range(NEAR)]


def slot_of(z, target):
    odd = lax.rem(target + Z - z, 2)
    base = z + odd * (1 - 2 * lax.rem(z, 2))
    return odd * HALF + lax.rem(target + Z - base, Z) // 2


def gelu_pair(pre):
    tanh_val = jnp.tanh(ROOT_COEFF * (pre + CUBIC_COEFF * pre * pre * pre))
    values = 0.5 * pre * (1.0 + tanh_val)
    slopes = 0.5 * (1.0 + tanh_val) + 0.5 * pre * (1.0 - tanh_val * tanh_val) * ROOT_COEFF * (
        1.0 + 3.0 * CUBIC_COEFF * pre * pre
    )
    return values, slopes


def dot(a, b, dims):
    return lax.dot_general(a, b, (dims, ((), ())), preferred_element_type=jnp.float32)


def place(lists, s):
    row, col = lists[0, s], lists[1, s]
    live = jnp.where(row >= 0, 1.0, 0.0).astype(jnp.float32)
    row = jnp.maximum(row, 0)
    return row, pl.multiple_of(jnp.maximum(col, 0) * BLK, BLK), live


def features(core, near, far):
    return pl.ds(pl.multiple_of(owner_at(core, near, far) * OWN, OWN), OWN)


def units_kernel(where, in_l, out_l, parts, w_in, w_out, keep, send, act, dh, xg, hidden, d_act):
    core, z = where[0], where[1]
    for near in range(NEAR):
        for far in range(FAR):
            xg[features(core, near, far), :] = parts[near, far]
    hidden[...] = jnp.zeros_like(hidden)
    d_act[...] = jnp.zeros_like(d_act)

    def product(s, carry):
        row, col, live = place(in_l, s)
        hidden[row] += dot(w_in[s], xg[pl.ds(col, BLK), :T], ((1,), (0,))) * live
        row, col, live = place(out_l, s)
        d_act[row] += dot(w_out[s], xg[pl.ds(col, BLK), T:], ((1,), (0,))) * live
        return carry

    lax.fori_loop(0, CAP, product, 0, unroll=8)
    for row in range(ROWS):
        values, slopes = gelu_pair(hidden[row])
        act[row] = values.astype(act.dtype)
        dh[row] = (d_act[row] * slopes).astype(dh.dtype)

    first = core == 0
    scale = float(T * Z * C) ** -0.5
    slots = [
        [slot_of(lax.rem(z + Z - c, Z), lax.rem(target + Z - c, Z)) for target in range(Z)]
        for c in (core, 1 - core)
    ]

    def pair(p, carry):
        for which, (lists, units, lo) in enumerate(((out_l, act, T), (in_l, dh, 0))):
            two = []
            for i in range(2):
                row, col, live = place(lists, 2 * p + i)
                part = dot(units[row], xg[pl.ds(col, BLK), lo : lo + T], ((1,), (1,)))
                two.append((part * (live * scale)).reshape(Z, C, SUB, BLK))
            both = jnp.stack(two, axis=2).reshape(Z, C, 2 * SUB, BLK)
            at = pl.multiple_of((which * CAP + 2 * p) * SUB, 2 * SUB)
            mine = jnp.where(first, both[:, 0], both[:, 1]).astype(keep.dtype)
            others = jnp.where(first, both[:, 1], both[:, 0]).astype(send.dtype)
            for target in range(Z):
                keep[slots[0][target], pl.ds(at, 2 * SUB), :] = mine[target]
                send[slots[1][target], pl.ds(at, 2 * SUB), :] = others[target]
        return carry

    lax.fori_loop(0, CAP // 2, pair, 0, unroll=4)


def add_products(lists, units, weights, total):
    total[...] = jnp.zeros_like(total)

    def product(s, carry):
        row, col, live = place(lists, s)
        total[pl.ds(col, BLK), :] += dot(weights[s], units[row], ((0,), (0,))) * live
        return carry

    lax.fori_loop(0, CAP, product, 0, unroll=8)


def output_kernel(lists, act, w_out, part, total):
    add_products(lists, act, w_out, total)
    part[...] = total[...].astype(part.dtype)


def partials_kernel(where, lists, dh, w_in, y_part, parts, total):
    add_products(lists, dh, w_in, total)
    for near in range(NEAR):
        for far in range(FAR):
            rows = features(where[0], near, far)
            parts[near, far, :, :T] = y_part[rows, :]
            parts[near, far, :, T:] = total[rows, :].astype(parts.dtype)


def cores_kernel(keep, got, near, far):
    for slot in range(Z):
        both = keep[slot].astype(jnp.float32) + got[slot].astype(jnp.float32)
        out = near if slot < HALF else far
        out[slot % HALF] = both.astype(out.dtype)


def pairs_kernel(near, got, *outs):
    for slot, out in enumerate(outs):
        both = near[slot].astype(jnp.float32) + got[slot].astype(jnp.float32)
        out[...] = both.astype(out.dtype)


def last_kernel(*refs):
    *moved, out_grad, in_grad = refs
    rows = CAP * SUB
    for i, grad in enumerate((out_grad, in_grad)):
        part = slice(i * rows, (i + 1) * rows)
        grad[...] = sum(m[part, :].astype(jnp.float32) for m in moved).astype(grad.dtype)


def near_sum_kernel(parts, out):
    for far in range(FAR):
        total = sum(parts[near, far].astype(jnp.float32) for near in range(NEAR))
        out[far] = total.astype(out.dtype)


def far_sum_kernel(parts, y, dx):
    total = sum(parts[far].astype(jnp.float32) for far in range(FAR)).astype(y.dtype)
    y[...] = total[:, :T]
    dx[...] = total[:, T:]


SMEM = pl.BlockSpec(memory_space=pltpu.SMEM)
VMEM = pl.BlockSpec(memory_space=pltpu.VMEM)
LIMIT = pltpu.CompilerParams(vmem_limit_bytes=24 * 1024 * 1024)
INTERPRET = False


def call(kernel, scalars, arrays, outs, scratch=()):
    bf = jnp.bfloat16
    return pl.pallas_call(
        kernel,
        out_shape=tuple(jax.ShapeDtypeStruct(dims, bf) for dims in outs),
        in_specs=[SMEM] * len(scalars) + [VMEM] * len(arrays),
        out_specs=[VMEM] * len(outs),
        scratch_shapes=[pltpu.VMEM(*dims) for dims in scratch],
        compiler_params=LIMIT,
        interpret=INTERPRET,
    )(*scalars, *arrays)


def units_call(where, in_l, out_l, parts, w_in, w_out):
    f32 = jnp.float32
    scratch = (((FEAT, 2 * T), jnp.bfloat16), (UNITS, f32), (UNITS, f32))
    outs = ((Z,) + STEP, (Z,) + STEP, UNITS, UNITS)
    return call(units_kernel, (where, in_l, out_l), (parts, w_in, w_out), outs, scratch)


def output_call(lists, act, w_out):
    scratch = (((FEAT, T), jnp.float32),)
    return call(output_kernel, (lists,), (act, w_out), ((FEAT, T),), scratch)[0]


def partials_call(where, lists, dh, w_in, y_part):
    scratch = (((FEAT, T), jnp.float32),)
    outs = ((NEAR, FAR, OWN, 2 * T),)
    return call(partials_kernel, (where, lists), (dh, w_in, y_part), outs, scratch)[0]


def exchange(x, groups):
    return lax.all_to_all(
        x, ("c", "x", "y"), split_axis=0, concat_axis=0, axis_index_groups=groups
    )


def spread(x, groups):
    return exchange(jnp.broadcast_to(x[None], (len(groups[0]),) + x.shape), groups)


def neighbour(z, c):
    return ((z - c) % Z ^ 1) + c


def body(tokens, cotangent, in_blocks, in_lists, out_blocks, out_lists):
    in_l, out_l = in_lists.T, out_lists.T
    own = jnp.concatenate([tokens.T, cotangent.T], axis=1)
    where = jnp.stack([lax.axis_index("c"), lax.axis_index("z")]).astype(jnp.int32)
    own, where = lax.optimization_barrier((own, where))
    parts = spread(spread(own, FAR_GROUPS), NEAR_GROUPS)
    keep, send, act, dh = units_call(where, in_l, out_l, parts, in_blocks, out_blocks)
    got = lax.ppermute(send, "c", [(0, 1), (1, 0)])
    y_part = output_call(out_l, act, out_blocks)
    y_part, got = lax.optimization_barrier((y_part, got))
    near, far = call(cores_kernel, (), (keep, got), ((HALF,) + STEP,) * 2)
    near, far, dh = lax.optimization_barrier((near, far, dh))
    pairs = [
        (z * C + c, neighbour(z, c) % Z * C + c) for z in range(Z) for c in range(C)
    ]
    got = lax.ppermute(far, ("z", "c"), pairs)
    parts = partials_call(where, in_l, dh, in_blocks, y_part)
    parts = exchange(parts, NEAR_GROUPS)
    own, *steps = call(pairs_kernel, (), (near, got), (STEP,) * HALF)
    moved = [
        lax.ppermute(step, "z", [(z, (z + 2 * k) % Z) for z in range(Z)])
        for k, step in enumerate(steps, 1)
    ]
    parts, moved[0], moved[1] = lax.optimization_barrier((parts, moved[0], moved[1]))
    (parts,) = call(near_sum_kernel, (), (parts,), ((FAR, OWN, 2 * T),))
    parts = exchange(parts, FAR_GROUPS)
    y, dx = call(far_sum_kernel, (), (parts,), ((OWN, T),) * 2)
    grads = call(last_kernel, (), (own, *moved), ((CAP * SUB, BLK),) * 2)
    out_grad, in_grad = (grad.reshape(CAP, SUB, BLK) for grad in grads)
    return y.T, dx.T, in_grad, out_grad


def solution(mesh):
    fine = Mesh(mesh.devices.reshape(Z, C, X, Y), ("z", "c", "x", "y"))
    dp, mp = ("z", "c"), ("x", "y")
    blocks, lists = P(mp, None, None), P(mp, None)
    return jax.shard_map(
        body,
        mesh=fine,
        in_specs=(P(dp, mp), P(dp, mp), blocks, lists, blocks, lists),
        out_specs=(P(dp, mp), P(dp, mp), P(mp, dp, None), P(mp, dp, None)),
        check_vma=False,
    )
```

```python
import math

import jax
import jax.numpy as jnp
from jax import lax
from jax.experimental import pallas as pl
from jax.experimental.pallas import tpu as pltpu
from jax.sharding import Mesh
from jax.sharding import PartitionSpec as P

Z, C, X, Y = 8, 2, 4, 8
BLK = 128
CAP = 32
ROWS = 5
COLS = 20
T = 256
FEAT = COLS * BLK
OWN = FEAT // (X * Y)
SUB = BLK // (Z * C)
NEAR = 4
FAR = X * Y // NEAR
HALF = Z // 2
UNITS = (ROWS, BLK, T)
STEP = (2 * CAP * SUB, BLK)

ROOT_COEFF = math.sqrt(2.0 / math.pi)
CUBIC_COEFF = 0.044715


def owner_at(core, near, far):
    x = lax.rem(2 * (far // (Y // 2)) + near // 2 + core, X)
    y = lax.rem(2 * (far % (Y // 2)) + near % 2 + core, Y)
    return x * Y + y


def device_at(core, near, far):
    x = (2 * (far // (Y // 2)) + near // 2 + core) % X
    y = (2 * (far % (Y // 2)) + near % 2 + core) % Y
    return (core * X + x) * Y + y


NEAR_GROUPS = [[device_at(c, n, f) for n in range(NEAR)] for c in range(C) for f in range(FAR)]
FAR_GROUPS = [[device_at(c, n, f) for f in range(FAR)] for c in range(C) for n in range(NEAR)]


def slot_of(z, target):
    odd = lax.rem(target + Z - z, 2)
    base = z + odd * (1 - 2 * lax.rem(z, 2))
    return odd * HALF + lax.rem(target + Z - base, Z) // 2


def gelu_pair(pre):
    tanh_val = jnp.tanh(ROOT_COEFF * (pre + CUBIC_COEFF * pre * pre * pre))
    values = 0.5 * pre * (1.0 + tanh_val)
    slopes = 0.5 * (1.0 + tanh_val) + 0.5 * pre * (1.0 - tanh_val * tanh_val) * ROOT_COEFF * (
        1.0 + 3.0 * CUBIC_COEFF * pre * pre
    )
    return values, slopes


def dot(a, b, dims):
    return lax.dot_general(a, b, (dims, ((), ())), preferred_element_type=jnp.float32)


def place(lists, s):
    row, col = lists[0, s], lists[1, s]
    live = jnp.where(row >= 0, 1.0, 0.0).astype(jnp.float32)
    row = jnp.maximum(row, 0)
    return row, pl.multiple_of(jnp.maximum(col, 0) * BLK, BLK), live


def features(core, near, far):
    return pl.ds(pl.multiple_of(owner_at(core, near, far) * OWN, OWN), OWN)


def units_kernel(where, in_l, out_l, parts, w_in, w_out, keep, send, act, dh, xg, hidden, d_act):
    core, z = where[0], where[1]
    for near in range(NEAR):
        for far in range(FAR):
            xg[features(core, near, far), :] = parts[near, far]
    hidden[...] = jnp.zeros_like(hidden)
    d_act[...] = jnp.zeros_like(d_act)

    def product(s, carry):
        row, col, live = place(in_l, s)
        hidden[row] += dot(w_in[s], xg[pl.ds(col, BLK), :T], ((1,), (0,))) * live
        row, col, live = place(out_l, s)
        d_act[row] += dot(w_out[s], xg[pl.ds(col, BLK), T:], ((1,), (0,))) * live
        return carry

    lax.fori_loop(0, CAP, product, 0, unroll=8)
    for row in range(ROWS):
        values, slopes = gelu_pair(hidden[row])
        act[row] = values.astype(act.dtype)
        dh[row] = (d_act[row] * slopes).astype(dh.dtype)

    first = core == 0
    scale = float(T * Z * C) ** -0.5
    slots = [
        [slot_of(lax.rem(z + Z - c, Z), lax.rem(target + Z - c, Z)) for target in range(Z)]
        for c in (core, 1 - core)
    ]

    def pair(p, carry):
        for which, (lists, units, lo) in enumerate(((out_l, act, T), (in_l, dh, 0))):
            two = []
            for i in range(2):
                row, col, live = place(lists, 2 * p + i)
                part = dot(units[row], xg[pl.ds(col, BLK), lo : lo + T], ((1,), (1,)))
                two.append((part * (live * scale)).reshape(Z, C, SUB, BLK))
            both = jnp.stack(two, axis=2).reshape(Z, C, 2 * SUB, BLK)
            at = pl.multiple_of((which * CAP + 2 * p) * SUB, 2 * SUB)
            mine = jnp.where(first, both[:, 0], both[:, 1]).astype(keep.dtype)
            others = jnp.where(first, both[:, 1], both[:, 0]).astype(send.dtype)
            for target in range(Z):
                keep[slots[0][target], pl.ds(at, 2 * SUB), :] = mine[target]
                send[slots[1][target], pl.ds(at, 2 * SUB), :] = others[target]
        return carry

    lax.fori_loop(0, CAP // 2, pair, 0, unroll=4)


def add_products(lists, units, weights, total):
    total[...] = jnp.zeros_like(total)

    def product(s, carry):
        row, col, live = place(lists, s)
        total[pl.ds(col, BLK), :] += dot(weights[s], units[row], ((0,), (0,))) * live
        return carry

    lax.fori_loop(0, CAP, product, 0, unroll=8)


def output_kernel(lists, act, w_out, part, total):
    add_products(lists, act, w_out, total)
    part[...] = total[...].astype(part.dtype)


def partials_kernel(where, lists, dh, w_in, y_part, parts, total):
    add_products(lists, dh, w_in, total)
    for near in range(NEAR):
        for far in range(FAR):
            rows = features(where[0], near, far)
            parts[near, far, :, :T] = y_part[rows, :]
            parts[near, far, :, T:] = total[rows, :].astype(parts.dtype)


def cores_kernel(keep, got, near, far):
    for slot in range(Z):
        both = keep[slot].astype(jnp.float32) + got[slot].astype(jnp.float32)
        out = near if slot < HALF else far
        out[slot % HALF] = both.astype(out.dtype)


def pairs_kernel(near, got, *outs):
    for slot, out in enumerate(outs):
        both = near[slot].astype(jnp.float32) + got[slot].astype(jnp.float32)
        out[...] = both.astype(out.dtype)


def last_kernel(*refs):
    *moved, out_grad, in_grad = refs
    rows = CAP * SUB
    for i, grad in enumerate((out_grad, in_grad)):
        part = slice(i * rows, (i + 1) * rows)
        grad[...] = sum(m[part, :].astype(jnp.float32) for m in moved).astype(grad.dtype)


def near_sum_kernel(parts, out):
    for far in range(FAR):
        total = sum(parts[near, far].astype(jnp.float32) for near in range(NEAR))
        out[far] = total.astype(out.dtype)


def far_sum_kernel(parts, y, dx):
    total = sum(parts[far].astype(jnp.float32) for far in range(FAR)).astype(y.dtype)
    y[...] = total[:, :T]
    dx[...] = total[:, T:]


SMEM = pl.BlockSpec(memory_space=pltpu.SMEM)
VMEM = pl.BlockSpec(memory_space=pltpu.VMEM)
LIMIT = pltpu.CompilerParams(vmem_limit_bytes=24 * 1024 * 1024)
INTERPRET = False


def call(kernel, scalars, arrays, outs, scratch=()):
    bf = jnp.bfloat16
    return pl.pallas_call(
        kernel,
        out_shape=tuple(jax.ShapeDtypeStruct(dims, bf) for dims in outs),
        in_specs=[SMEM] * len(scalars) + [VMEM] * len(arrays),
        out_specs=[VMEM] * len(outs),
        scratch_shapes=[pltpu.VMEM(*dims) for dims in scratch],
        compiler_params=LIMIT,
        interpret=INTERPRET,
    )(*scalars, *arrays)


def units_call(where, in_l, out_l, parts, w_in, w_out):
    f32 = jnp.float32
    scratch = (((FEAT, 2 * T), jnp.bfloat16), (UNITS, f32), (UNITS, f32))
    outs = ((Z,) + STEP, (Z,) + STEP, UNITS, UNITS)
    return call(units_kernel, (where, in_l, out_l), (parts, w_in, w_out), outs, scratch)


def output_call(lists, act, w_out):
    scratch = (((FEAT, T), jnp.float32),)
    return call(output_kernel, (lists,), (act, w_out), ((FEAT, T),), scratch)[0]


def partials_call(where, lists, dh, w_in, y_part):
    scratch = (((FEAT, T), jnp.float32),)
    outs = ((NEAR, FAR, OWN, 2 * T),)
    return call(partials_kernel, (where, lists), (dh, w_in, y_part), outs, scratch)[0]


def exchange(x, groups):
    return lax.all_to_all(
        x, ("c", "x", "y"), split_axis=0, concat_axis=0, axis_index_groups=groups
    )


def spread(x, groups):
    return exchange(jnp.broadcast_to(x[None], (len(groups[0]),) + x.shape), groups)


def neighbour(z, c):
    return ((z - c) % Z ^ 1) + c


def body(tokens, cotangent, in_blocks, in_lists, out_blocks, out_lists):
    in_l, out_l = in_lists.T, out_lists.T
    own = jnp.concatenate([tokens.T, cotangent.T], axis=1)
    where = jnp.stack([lax.axis_index("c"), lax.axis_index("z")]).astype(jnp.int32)
    own, where = lax.optimization_barrier((own, where))
    parts = spread(spread(own, FAR_GROUPS), NEAR_GROUPS)
    keep, send, act, dh = units_call(where, in_l, out_l, parts, in_blocks, out_blocks)
    got = lax.ppermute(send, "c", [(0, 1), (1, 0)])
    y_part = output_call(out_l, act, out_blocks)
    y_part, got = lax.optimization_barrier((y_part, got))
    near, far = call(cores_kernel, (), (keep, got), ((HALF,) + STEP,) * 2)
    near, far, dh = lax.optimization_barrier((near, far, dh))
    pairs = [
        (z * C + c, neighbour(z, c) % Z * C + c) for z in range(Z) for c in range(C)
    ]
    got = lax.ppermute(far, ("z", "c"), pairs)
    parts = partials_call(where, in_l, dh, in_blocks, y_part)
    parts = exchange(parts, NEAR_GROUPS)
    own, *steps = call(pairs_kernel, (), (near, got), (STEP,) * HALF)
    moved = [
        lax.ppermute(step, "z", [(z, (z + 2 * k) % Z) for z in range(Z)])
        for k, step in enumerate(steps, 1)
    ]
    parts, moved[1] = lax.optimization_barrier((parts, moved[1]))
    (parts,) = call(near_sum_kernel, (), (parts,), ((FAR, OWN, 2 * T),))
    parts = exchange(parts, FAR_GROUPS)
    y, dx = call(far_sum_kernel, (), (parts,), ((OWN, T),) * 2)
    grads = call(last_kernel, (), (own, *moved), ((CAP * SUB, BLK),) * 2)
    out_grad, in_grad = (grad.reshape(CAP, SUB, BLK) for grad in grads)
    return y.T, dx.T, in_grad, out_grad


def solution(mesh):
    fine = Mesh(mesh.devices.reshape(Z, C, X, Y), ("z", "c", "x", "y"))
    dp, mp = ("z", "c"), ("x", "y")
    blocks, lists = P(mp, None, None), P(mp, None)
    return jax.shard_map(
        body,
        mesh=fine,
        in_specs=(P(dp, mp), P(dp, mp), blocks, lists, blocks, lists),
        out_specs=(P(dp, mp), P(dp, mp), P(mp, dp, None), P(mp, dp, None)),
        check_vma=False,
    )
```

```python
import math

import jax
import jax.numpy as jnp
from jax import lax
from jax.experimental import pallas as pl
from jax.experimental.pallas import tpu as pltpu
from jax.sharding import Mesh
from jax.sharding import PartitionSpec as P

Z, C, X, Y = 8, 2, 4, 8
BLK = 128
CAP = 32
ROWS = 5
COLS = 20
T = 256
FEAT = COLS * BLK
OWN = FEAT // (X * Y)
SUB = BLK // (Z * C)
NEAR = 4
FAR = X * Y // NEAR
HALF = Z // 2
UNITS = (ROWS, BLK, T)
STEP = (2 * CAP * SUB, BLK)

ROOT_COEFF = math.sqrt(2.0 / math.pi)
CUBIC_COEFF = 0.044715


def owner_at(core, near, far):
    x = lax.rem(2 * (far // (Y // 2)) + near // 2 + core, X)
    y = lax.rem(2 * (far % (Y // 2)) + near % 2 + core, Y)
    return x * Y + y


def device_at(core, near, far):
    x = (2 * (far // (Y // 2)) + near // 2 + core) % X
    y = (2 * (far % (Y // 2)) + near % 2 + core) % Y
    return (core * X + x) * Y + y


NEAR_GROUPS = [[device_at(c, n, f) for n in range(NEAR)] for c in range(C) for f in range(FAR)]
FAR_GROUPS = [[device_at(c, n, f) for f in range(FAR)] for c in range(C) for n in range(NEAR)]


def slot_of(z, target):
    odd = lax.rem(target + Z - z, 2)
    base = z + odd * (1 - 2 * lax.rem(z, 2))
    return odd * HALF + lax.rem(target + Z - base, Z) // 2


def gelu_pair(pre):
    tanh_val = jnp.tanh(ROOT_COEFF * (pre + CUBIC_COEFF * pre * pre * pre))
    values = 0.5 * pre * (1.0 + tanh_val)
    slopes = 0.5 * (1.0 + tanh_val) + 0.5 * pre * (1.0 - tanh_val * tanh_val) * ROOT_COEFF * (
        1.0 + 3.0 * CUBIC_COEFF * pre * pre
    )
    return values, slopes


def dot(a, b, dims):
    return lax.dot_general(a, b, (dims, ((), ())), preferred_element_type=jnp.float32)


def place(lists, s):
    row, col = lists[0, s], lists[1, s]
    live = jnp.where(row >= 0, 1.0, 0.0).astype(jnp.float32)
    row = jnp.maximum(row, 0)
    return row, pl.multiple_of(jnp.maximum(col, 0) * BLK, BLK), live


def features(core, near, far):
    return pl.ds(pl.multiple_of(owner_at(core, near, far) * OWN, OWN), OWN)


def gather_features(core, parts, xg):
    for near in range(NEAR):
        for far in range(FAR):
            xg[features(core, near, far), :] = parts[near, far]


def partials_kernel(
    where, in_l, out_l, xg_parts, w_in, w_out, act, dh, parts, xg, hidden, d_act, y, dx, stage, sems
):
    core = where[0]
    gather_features(core, xg_parts, xg)
    for total in (hidden, d_act, y, dx):
        total[...] = jnp.zeros_like(total)

    def up(s, carry):
        row, col, live = place(in_l, s)
        hidden[row] += dot(w_in[s], xg[pl.ds(col, BLK), :T], ((1,), (0,))) * live
        row, col, live = place(out_l, s)
        d_act[row] += dot(w_out[s], xg[pl.ds(col, BLK), T:], ((1,), (0,))) * live
        return carry

    def down(s, carry):
        row, col, live = place(out_l, s)
        y[pl.ds(col, BLK), :] += dot(w_out[s], act[row], ((0,), (0,))) * live
        row, col, live = place(in_l, s)
        dx[pl.ds(col, BLK), :] += dot(w_in[s], dh[row], ((0,), (0,))) * live
        return carry

    lax.fori_loop(0, CAP, up, 0, unroll=8)
    for row in range(ROWS):
        values, slopes = gelu_pair(hidden[row])
        act[row] = values.astype(act.dtype)
        dh[row] = (d_act[row] * slopes).astype(dh.dtype)
    lax.fori_loop(0, CAP, down, 0, unroll=8)
    copies = []
    for near in range(NEAR):
        for far in range(FAR):
            rows = features(core, near, far)
            stage[near, far, :, :T] = y[rows, :].astype(stage.dtype)
            stage[near, far, :, T:] = dx[rows, :].astype(stage.dtype)
        copies.append(pltpu.make_async_copy(stage.at[near], parts.at[near], sems.at[near]))
        copies[-1].start()
    for copy in copies:
        copy.wait()


def grads_kernel(where, in_l, out_l, xg_parts, act, dh, keep, send, xg):
    core, z = where[0], where[1]
    gather_features(core, xg_parts, xg)
    first = core == 0
    scale = float(T * Z * C) ** -0.5
    slots = [
        [slot_of(lax.rem(z + Z - c, Z), lax.rem(target + Z - c, Z)) for target in range(Z)]
        for c in (core, 1 - core)
    ]

    def pair(p, carry):
        for which, (lists, units, lo) in enumerate(((out_l, act, T), (in_l, dh, 0))):
            two = []
            for i in range(2):
                row, col, live = place(lists, 2 * p + i)
                part = dot(units[row], xg[pl.ds(col, BLK), lo : lo + T], ((1,), (1,)))
                two.append((part * (live * scale)).reshape(Z, C, SUB, BLK))
            both = jnp.stack(two, axis=2).reshape(Z, C, 2 * SUB, BLK)
            at = pl.multiple_of((which * CAP + 2 * p) * SUB, 2 * SUB)
            mine = jnp.where(first, both[:, 0], both[:, 1]).astype(keep.dtype)
            others = jnp.where(first, both[:, 1], both[:, 0]).astype(send.dtype)
            for target in range(Z):
                keep[slots[0][target], pl.ds(at, 2 * SUB), :] = mine[target]
                send[slots[1][target], pl.ds(at, 2 * SUB), :] = others[target]
        return carry

    lax.fori_loop(0, CAP // 2, pair, 0, unroll=4)


def cores_kernel(keep, got, near, far):
    for slot in range(Z):
        both = keep[slot].astype(jnp.float32) + got[slot].astype(jnp.float32)
        out = near if slot < HALF else far
        out[slot % HALF] = both.astype(out.dtype)


def pairs_kernel(near, got, *outs):
    for slot, out in enumerate(outs):
        both = near[slot].astype(jnp.float32) + got[slot].astype(jnp.float32)
        out[...] = both.astype(out.dtype)


def last_kernel(*refs):
    *moved, out_grad, in_grad = refs
    rows = CAP * SUB
    for i, grad in enumerate((out_grad, in_grad)):
        part = slice(i * rows, (i + 1) * rows)
        grad[...] = sum(m[part, :].astype(jnp.float32) for m in moved).astype(grad.dtype)


def near_sum_kernel(parts, out):
    for far in range(FAR):
        total = sum(parts[near, far].astype(jnp.float32) for near in range(NEAR))
        out[far] = total.astype(out.dtype)


def far_sum_kernel(parts, y, dx):
    total = sum(parts[far].astype(jnp.float32) for far in range(FAR)).astype(y.dtype)
    y[...] = total[:, :T]
    dx[...] = total[:, T:]


SMEM = pl.BlockSpec(memory_space=pltpu.SMEM)
VMEM = pl.BlockSpec(memory_space=pltpu.VMEM)
LIMIT = pltpu.CompilerParams(vmem_limit_bytes=24 * 1024 * 1024)
INTERPRET = False


def call(kernel, scalars, arrays, outs, scratch=()):
    bf = jnp.bfloat16
    return pl.pallas_call(
        kernel,
        out_shape=tuple(jax.ShapeDtypeStruct(dims, bf) for dims in outs),
        in_specs=[SMEM] * len(scalars) + [VMEM] * len(arrays),
        out_specs=[VMEM] * len(outs),
        scratch_shapes=[pltpu.VMEM(*dims) for dims in scratch],
        compiler_params=LIMIT,
        interpret=INTERPRET,
    )(*scalars, *arrays)


def partials_call(where, in_l, out_l, xg_parts, w_in, w_out):
    bf, f32 = jnp.bfloat16, jnp.float32
    groups = (NEAR, FAR, OWN, 2 * T)
    return pl.pallas_call(
        partials_kernel,
        out_shape=(*[jax.ShapeDtypeStruct(UNITS, bf)] * 2, pltpu.HBM(groups, bf)),
        in_specs=[SMEM] * 3 + [VMEM] * 3,
        out_specs=(VMEM, VMEM, pl.BlockSpec(memory_space=pltpu.HBM)),
        scratch_shapes=[
            pltpu.VMEM((FEAT, 2 * T), bf),
            *[pltpu.VMEM(UNITS, f32)] * 2,
            *[pltpu.VMEM((FEAT, T), f32)] * 2,
            pltpu.VMEM(groups, bf),
            pltpu.SemaphoreType.DMA((NEAR,)),
        ],
        compiler_params=LIMIT,
        interpret=INTERPRET,
    )(where, in_l, out_l, xg_parts, w_in, w_out)


def grads_call(where, in_l, out_l, xg_parts, act, dh):
    scratch = (((FEAT, 2 * T), jnp.bfloat16),)
    outs = ((Z,) + STEP,) * 2
    return call(grads_kernel, (where, in_l, out_l), (xg_parts, act, dh), outs, scratch)


def exchange(x, groups):
    return lax.all_to_all(
        x, ("c", "x", "y"), split_axis=0, concat_axis=0, axis_index_groups=groups
    )


def spread(x, groups):
    return exchange(jnp.broadcast_to(x[None], (len(groups[0]),) + x.shape), groups)


def neighbour(z, c):
    return ((z - c) % Z ^ 1) + c


def body(tokens, cotangent, in_blocks, in_lists, out_blocks, out_lists):
    in_l, out_l = in_lists.T, out_lists.T
    own = jnp.concatenate([tokens.T, cotangent.T], axis=1)
    where = jnp.stack([lax.axis_index("c"), lax.axis_index("z")]).astype(jnp.int32)
    own, where = lax.optimization_barrier((own, where))
    xg = spread(spread(own, FAR_GROUPS), NEAR_GROUPS)
    act, dh, parts = partials_call(where, in_l, out_l, xg, in_blocks, out_blocks)
    parts = exchange(parts, NEAR_GROUPS)
    keep, send = grads_call(where, in_l, out_l, xg, act, dh)
    got = lax.ppermute(send, "c", [(0, 1), (1, 0)])
    near, far = call(cores_kernel, (), (keep, got), ((HALF,) + STEP,) * 2)
    pairs = [
        (z * C + c, neighbour(z, c) % Z * C + c) for z in range(Z) for c in range(C)
    ]
    got = lax.ppermute(far, ("z", "c"), pairs)
    parts, got = lax.optimization_barrier((parts, got))
    own, *steps = call(pairs_kernel, (), (near, got), (STEP,) * HALF)
    moved = [
        lax.ppermute(step, "z", [(z, (z + 2 * k) % Z) for z in range(Z)])
        for k, step in enumerate(steps, 1)
    ]
    (parts,) = call(near_sum_kernel, (), (parts,), ((FAR, OWN, 2 * T),))
    parts = exchange(parts, FAR_GROUPS)
    y, dx = call(far_sum_kernel, (), (parts,), ((OWN, T),) * 2)
    grads = call(last_kernel, (), (own, *moved), ((CAP * SUB, BLK),) * 2)
    out_grad, in_grad = (grad.reshape(CAP, SUB, BLK) for grad in grads)
    return y.T, dx.T, in_grad, out_grad


def solution(mesh):
    fine = Mesh(mesh.devices.reshape(Z, C, X, Y), ("z", "c", "x", "y"))
    dp, mp = ("z", "c"), ("x", "y")
    blocks, lists = P(mp, None, None), P(mp, None)
    return jax.shard_map(
        body,
        mesh=fine,
        in_specs=(P(dp, mp), P(dp, mp), blocks, lists, blocks, lists),
        out_specs=(P(dp, mp), P(dp, mp), P(mp, dp, None), P(mp, dp, None)),
        check_vma=False,
    )
```

```python
import math

import jax
import jax.numpy as jnp
from jax import lax
from jax.experimental import pallas as pl
from jax.experimental.pallas import tpu as pltpu
from jax.sharding import Mesh
from jax.sharding import PartitionSpec as P

Z, C, X, Y = 8, 2, 4, 8
BLK = 128
CAP = 32
ROWS = 5
COLS = 20
T = 256
FEAT = COLS * BLK
OWN = FEAT // (X * Y)
SUB = BLK // (Z * C)
NEAR = 4
FAR = X * Y // NEAR
HALF = Z // 2
UNITS = (ROWS, BLK, T)
STEP = (2 * CAP * SUB, BLK)

ROOT_COEFF = math.sqrt(2.0 / math.pi)
CUBIC_COEFF = 0.044715


def owner_at(core, near, far):
    x = lax.rem(2 * (far // (Y // 2)) + near // 2 + core, X)
    y = lax.rem(2 * (far % (Y // 2)) + near % 2 + core, Y)
    return x * Y + y


def device_at(core, near, far):
    x = (2 * (far // (Y // 2)) + near // 2 + core) % X
    y = (2 * (far % (Y // 2)) + near % 2 + core) % Y
    return (core * X + x) * Y + y


NEAR_GROUPS = [[device_at(c, n, f) for n in range(NEAR)] for c in range(C) for f in range(FAR)]
FAR_GROUPS = [[device_at(c, n, f) for f in range(FAR)] for c in range(C) for n in range(NEAR)]


def slot_of(z, target):
    odd = lax.rem(target + Z - z, 2)
    base = z + odd * (1 - 2 * lax.rem(z, 2))
    return odd * HALF + lax.rem(target + Z - base, Z) // 2


def gelu_pair(pre):
    tanh_val = jnp.tanh(ROOT_COEFF * (pre + CUBIC_COEFF * pre * pre * pre))
    values = 0.5 * pre * (1.0 + tanh_val)
    slopes = 0.5 * (1.0 + tanh_val) + 0.5 * pre * (1.0 - tanh_val * tanh_val) * ROOT_COEFF * (
        1.0 + 3.0 * CUBIC_COEFF * pre * pre
    )
    return values, slopes


def dot(a, b, dims):
    return lax.dot_general(a, b, (dims, ((), ())), preferred_element_type=jnp.float32)


def place(lists, s):
    row, col = lists[0, s], lists[1, s]
    live = jnp.where(row >= 0, 1.0, 0.0).astype(jnp.float32)
    row = jnp.maximum(row, 0)
    return row, pl.multiple_of(jnp.maximum(col, 0) * BLK, BLK), live


def features(core, near, far):
    return pl.ds(pl.multiple_of(owner_at(core, near, far) * OWN, OWN), OWN)


def gather_features(core, parts, xg):
    for near in range(NEAR):
        for far in range(FAR):
            xg[features(core, near, far), :] = parts[near, far]


def partials_kernel(
    where, in_l, out_l, xg_parts, w_in, w_out, act, dh, parts, xg, hidden, d_act, y, dx, stage, sems
):
    core = where[0]
    gather_features(core, xg_parts, xg)
    for total in (hidden, d_act, y, dx):
        total[...] = jnp.zeros_like(total)

    def up(s, carry):
        row, col, live = place(in_l, s)
        hidden[row] += dot(w_in[s], xg[pl.ds(col, BLK), :T], ((1,), (0,))) * live
        row, col, live = place(out_l, s)
        d_act[row] += dot(w_out[s], xg[pl.ds(col, BLK), T:], ((1,), (0,))) * live
        return carry

    def down(s, carry):
        row, col, live = place(out_l, s)
        y[pl.ds(col, BLK), :] += dot(w_out[s], act[row], ((0,), (0,))) * live
        row, col, live = place(in_l, s)
        dx[pl.ds(col, BLK), :] += dot(w_in[s], dh[row], ((0,), (0,))) * live
        return carry

    lax.fori_loop(0, CAP, up, 0, unroll=CAP)
    for row in range(ROWS):
        values, slopes = gelu_pair(hidden[row])
        act[row] = values.astype(act.dtype)
        dh[row] = (d_act[row] * slopes).astype(dh.dtype)
    lax.fori_loop(0, CAP, down, 0, unroll=CAP)
    copies = []
    for near in range(NEAR):
        for far in range(FAR):
            rows = features(core, near, far)
            stage[near, far, :, :T] = y[rows, :].astype(stage.dtype)
            stage[near, far, :, T:] = dx[rows, :].astype(stage.dtype)
        copies.append(pltpu.make_async_copy(stage.at[near], parts.at[near], sems.at[near]))
        copies[-1].start()
    for copy in copies:
        copy.wait()


def grads_kernel(where, in_l, out_l, xg_parts, act, dh, keep, send, xg):
    core, z = where[0], where[1]
    gather_features(core, xg_parts, xg)
    first = core == 0
    scale = float(T * Z * C) ** -0.5
    slots = [
        [slot_of(lax.rem(z + Z - c, Z), lax.rem(target + Z - c, Z)) for target in range(Z)]
        for c in (core, 1 - core)
    ]

    def pair(p, carry):
        for which, (lists, units, lo) in enumerate(((out_l, act, T), (in_l, dh, 0))):
            two = []
            for i in range(2):
                row, col, live = place(lists, 2 * p + i)
                part = dot(units[row], xg[pl.ds(col, BLK), lo : lo + T], ((1,), (1,)))
                two.append((part * (live * scale)).reshape(Z, C, SUB, BLK))
            both = jnp.stack(two, axis=2).reshape(Z, C, 2 * SUB, BLK)
            at = pl.multiple_of((which * CAP + 2 * p) * SUB, 2 * SUB)
            mine = jnp.where(first, both[:, 0], both[:, 1]).astype(keep.dtype)
            others = jnp.where(first, both[:, 1], both[:, 0]).astype(send.dtype)
            for target in range(Z):
                keep[slots[0][target], pl.ds(at, 2 * SUB), :] = mine[target]
                send[slots[1][target], pl.ds(at, 2 * SUB), :] = others[target]
        return carry

    lax.fori_loop(0, CAP // 2, pair, 0, unroll=4)


def cores_kernel(keep, got, near, far):
    for slot in range(Z):
        both = keep[slot].astype(jnp.float32) + got[slot].astype(jnp.float32)
        out = near if slot < HALF else far
        out[slot % HALF] = both.astype(out.dtype)


def pairs_kernel(near, got, *outs):
    for slot, out in enumerate(outs):
        both = near[slot].astype(jnp.float32) + got[slot].astype(jnp.float32)
        out[...] = both.astype(out.dtype)


def last_kernel(*refs):
    *moved, out_grad, in_grad = refs
    rows = CAP * SUB
    for i, grad in enumerate((out_grad, in_grad)):
        part = slice(i * rows, (i + 1) * rows)
        grad[...] = sum(m[part, :].astype(jnp.float32) for m in moved).astype(grad.dtype)


def near_sum_kernel(parts, out):
    total = sum(parts[near].astype(jnp.float32) for near in range(NEAR))
    out[...] = total.astype(out.dtype)


def far_sum_kernel(parts, y, dx):
    total = sum(parts[far].astype(jnp.float32) for far in range(FAR)).astype(y.dtype)
    y[...] = total[:, :T]
    dx[...] = total[:, T:]


SMEM = pl.BlockSpec(memory_space=pltpu.SMEM)
VMEM = pl.BlockSpec(memory_space=pltpu.VMEM)
LIMIT = pltpu.CompilerParams(vmem_limit_bytes=24 * 1024 * 1024)
INTERPRET = False


def call(kernel, scalars, arrays, outs, scratch=()):
    bf = jnp.bfloat16
    return pl.pallas_call(
        kernel,
        out_shape=tuple(jax.ShapeDtypeStruct(dims, bf) for dims in outs),
        in_specs=[SMEM] * len(scalars) + [VMEM] * len(arrays),
        out_specs=[VMEM] * len(outs),
        scratch_shapes=[pltpu.VMEM(*dims) for dims in scratch],
        compiler_params=LIMIT,
        interpret=INTERPRET,
    )(*scalars, *arrays)


def partials_call(where, in_l, out_l, xg_parts, w_in, w_out):
    bf, f32 = jnp.bfloat16, jnp.float32
    groups = (NEAR, FAR, OWN, 2 * T)
    return pl.pallas_call(
        partials_kernel,
        out_shape=(*[jax.ShapeDtypeStruct(UNITS, bf)] * 2, pltpu.HBM(groups, bf)),
        in_specs=[SMEM] * 3 + [VMEM] * 3,
        out_specs=(VMEM, VMEM, pl.BlockSpec(memory_space=pltpu.HBM)),
        scratch_shapes=[
            pltpu.VMEM((FEAT, 2 * T), bf),
            *[pltpu.VMEM(UNITS, f32)] * 2,
            *[pltpu.VMEM((FEAT, T), f32)] * 2,
            pltpu.VMEM(groups, bf),
            pltpu.SemaphoreType.DMA((NEAR,)),
        ],
        compiler_params=LIMIT,
        interpret=INTERPRET,
    )(where, in_l, out_l, xg_parts, w_in, w_out)


def grads_call(where, in_l, out_l, xg_parts, act, dh):
    scratch = (((FEAT, 2 * T), jnp.bfloat16),)
    outs = ((Z,) + STEP,) * 2
    return call(grads_kernel, (where, in_l, out_l), (xg_parts, act, dh), outs, scratch)


def near_sum_call(parts):
    block = (2, OWN, 2 * T)
    return pl.pallas_call(
        near_sum_kernel,
        grid=(FAR // block[0],),
        out_shape=jax.ShapeDtypeStruct(parts.shape[1:], parts.dtype),
        in_specs=[pl.BlockSpec((NEAR,) + block, lambda i: (0, i, 0, 0))],
        out_specs=pl.BlockSpec(block, lambda i: (i, 0, 0)),
        compiler_params=LIMIT,
        interpret=INTERPRET,
    )(parts)


def exchange(x, groups):
    return lax.all_to_all(
        x, ("c", "x", "y"), split_axis=0, concat_axis=0, axis_index_groups=groups
    )


def spread(x, groups):
    return exchange(jnp.broadcast_to(x[None], (len(groups[0]),) + x.shape), groups)


def neighbour(z, c):
    return ((z - c) % Z ^ 1) + c


def body(tokens, cotangent, in_blocks, in_lists, out_blocks, out_lists):
    in_l, out_l = in_lists.T, out_lists.T
    own = jnp.concatenate([tokens.T, cotangent.T], axis=1)
    where = jnp.stack([lax.axis_index("c"), lax.axis_index("z")]).astype(jnp.int32)
    own, where = lax.optimization_barrier((own, where))
    xg = spread(spread(own, FAR_GROUPS), NEAR_GROUPS)
    act, dh, parts = partials_call(where, in_l, out_l, xg, in_blocks, out_blocks)
    parts = exchange(parts, NEAR_GROUPS)
    keep, send = grads_call(where, in_l, out_l, xg, act, dh)
    got = lax.ppermute(send, "c", [(0, 1), (1, 0)])
    near, far = call(cores_kernel, (), (keep, got), ((HALF,) + STEP,) * 2)
    pairs = [
        (z * C + c, neighbour(z, c) % Z * C + c) for z in range(Z) for c in range(C)
    ]
    got = lax.ppermute(far, ("z", "c"), pairs)
    parts, got = lax.optimization_barrier((parts, got))
    own, *steps = call(pairs_kernel, (), (near, got), (STEP,) * HALF)
    moved = [
        lax.ppermute(steps[k - 1], "z", [(z, (z + 2 * k) % Z) for z in range(Z)])
        for k in (2, 1, 3)
    ]
    parts = exchange(near_sum_call(parts), FAR_GROUPS)
    y, dx = call(far_sum_kernel, (), (parts,), ((OWN, T),) * 2)
    grads = call(last_kernel, (), (own, *moved), ((CAP * SUB, BLK),) * 2)
    out_grad, in_grad = (grad.reshape(CAP, SUB, BLK) for grad in grads)
    return y.T, dx.T, in_grad, out_grad


def solution(mesh):
    fine = Mesh(mesh.devices.reshape(Z, C, X, Y), ("z", "c", "x", "y"))
    dp, mp = ("z", "c"), ("x", "y")
    blocks, lists = P(mp, None, None), P(mp, None)
    return jax.shard_map(
        body,
        mesh=fine,
        in_specs=(P(dp, mp), P(dp, mp), blocks, lists, blocks, lists),
        out_specs=(P(dp, mp), P(dp, mp), P(mp, dp, None), P(mp, dp, None)),
        check_vma=False,
    )
```

```python
import math

import jax
import jax.numpy as jnp
from jax import lax
from jax.experimental import pallas as pl
from jax.experimental.pallas import tpu as pltpu
from jax.sharding import Mesh
from jax.sharding import PartitionSpec as P

Z, C, X, Y = 8, 2, 4, 8
BLK = 128
CAP = 32
ROWS = 5
COLS = 20
T = 256
FEAT = COLS * BLK
OWN = FEAT // (X * Y)
SUB = BLK // (Z * C)
NEAR = 4
FAR = X * Y // NEAR
HALF = Z // 2
UNITS = (ROWS, BLK, T)
STEP = (2 * CAP * SUB, BLK)

ROOT_COEFF = math.sqrt(2.0 / math.pi)
CUBIC_COEFF = 0.044715


def owner_at(core, near, far):
    x = lax.rem(2 * (far // (Y // 2)) + near // 2 + core, X)
    y = lax.rem(2 * (far % (Y // 2)) + near % 2 + core, Y)
    return x * Y + y


def device_at(core, near, far):
    x = (2 * (far // (Y // 2)) + near // 2 + core) % X
    y = (2 * (far % (Y // 2)) + near % 2 + core) % Y
    return (core * X + x) * Y + y


NEAR_GROUPS = [[device_at(c, n, f) for n in range(NEAR)] for c in range(C) for f in range(FAR)]
FAR_GROUPS = [[device_at(c, n, f) for f in range(FAR)] for c in range(C) for n in range(NEAR)]


def slot_of(z, target):
    odd = lax.rem(target + Z - z, 2)
    base = z + odd * (1 - 2 * lax.rem(z, 2))
    return odd * HALF + lax.rem(target + Z - base, Z) // 2


def gelu_pair(pre):
    tanh_val = jnp.tanh(ROOT_COEFF * (pre + CUBIC_COEFF * pre * pre * pre))
    values = 0.5 * pre * (1.0 + tanh_val)
    slopes = 0.5 * (1.0 + tanh_val) + 0.5 * pre * (1.0 - tanh_val * tanh_val) * ROOT_COEFF * (
        1.0 + 3.0 * CUBIC_COEFF * pre * pre
    )
    return values, slopes


def dot(a, b, dims):
    return lax.dot_general(a, b, (dims, ((), ())), preferred_element_type=jnp.float32)


def place(lists, s):
    row, col = lists[0, s], lists[1, s]
    live = jnp.where(row >= 0, 1.0, 0.0).astype(jnp.float32)
    row = jnp.maximum(row, 0)
    return row, pl.multiple_of(jnp.maximum(col, 0) * BLK, BLK), live


def features(core, near, far):
    return pl.ds(pl.multiple_of(owner_at(core, near, far) * OWN, OWN), OWN)


def gather_features(core, parts, xg):
    for near in range(NEAR):
        for far in range(FAR):
            xg[features(core, near, far), :] = parts[near, far]


def partials_kernel(
    where, in_l, out_l, xg_parts, w_in, w_out, act, dh, parts, xg, hidden, d_act, y, dx, sems
):
    core = where[0]
    gather_features(core, xg_parts, xg)
    for total in (hidden, d_act, y, dx):
        total[...] = jnp.zeros_like(total)

    def up(s, carry):
        row, col, live = place(in_l, s)
        hidden[row] += dot(w_in[s], xg[pl.ds(col, BLK), :T], ((1,), (0,))) * live
        row, col, live = place(out_l, s)
        d_act[row] += dot(w_out[s], xg[pl.ds(col, BLK), T:], ((1,), (0,))) * live
        return carry

    def down(s, carry):
        row, col, live = place(out_l, s)
        y[pl.ds(col, BLK), :] += dot(w_out[s], act[row], ((0,), (0,))) * live
        row, col, live = place(in_l, s)
        dx[pl.ds(col, BLK), :] += dot(w_in[s], dh[row], ((0,), (0,))) * live
        return carry

    lax.fori_loop(0, CAP, up, 0, unroll=CAP)
    for row in range(ROWS):
        values, slopes = gelu_pair(hidden[row])
        act[row] = values.astype(act.dtype)
        dh[row] = (d_act[row] * slopes).astype(dh.dtype)
    lax.fori_loop(0, CAP, down, 0, unroll=CAP)
    stage = xg.reshape(NEAR, FAR, OWN, 2 * T)
    copies = []
    for near in range(NEAR):
        for far in range(FAR):
            rows = features(core, near, far)
            stage[near, far, :, :T] = y[rows, :].astype(stage.dtype)
            stage[near, far, :, T:] = dx[rows, :].astype(stage.dtype)
        copies.append(pltpu.make_async_copy(stage.at[near], parts.at[near], sems.at[near]))
        copies[-1].start()
    for copy in copies:
        copy.wait()


def grads_kernel(where, in_l, out_l, xg_parts, act, dh, keep, send, xg):
    core, z = where[0], where[1]
    gather_features(core, xg_parts, xg)
    first = core == 0
    scale = float(T * Z * C) ** -0.5
    slots = [
        [slot_of(lax.rem(z + Z - c, Z), lax.rem(target + Z - c, Z)) for target in range(Z)]
        for c in (core, 1 - core)
    ]

    def pair(p, carry):
        for which, (lists, units, lo) in enumerate(((out_l, act, T), (in_l, dh, 0))):
            two = []
            for i in range(2):
                row, col, live = place(lists, 2 * p + i)
                part = dot(units[row], xg[pl.ds(col, BLK), lo : lo + T], ((1,), (1,)))
                two.append((part * (live * scale)).reshape(Z, C, SUB, BLK))
            both = jnp.stack(two, axis=2).reshape(Z, C, 2 * SUB, BLK)
            at = pl.multiple_of((which * CAP + 2 * p) * SUB, 2 * SUB)
            mine = jnp.where(first, both[:, 0], both[:, 1]).astype(keep.dtype)
            others = jnp.where(first, both[:, 1], both[:, 0]).astype(send.dtype)
            for target in range(Z):
                keep[slots[0][target], pl.ds(at, 2 * SUB), :] = mine[target]
                send[slots[1][target], pl.ds(at, 2 * SUB), :] = others[target]
        return carry

    lax.fori_loop(0, CAP // 2, pair, 0, unroll=CAP // 2)


def cores_kernel(keep, got, near, far):
    for slot in range(Z):
        both = keep[slot].astype(jnp.float32) + got[slot].astype(jnp.float32)
        out = near if slot < HALF else far
        out[slot % HALF] = both.astype(out.dtype)


def pairs_kernel(near, got, *outs):
    for slot, out in enumerate(outs):
        both = near[slot].astype(jnp.float32) + got[slot].astype(jnp.float32)
        out[...] = both.astype(out.dtype)


def last_kernel(*refs):
    *moved, out_grad, in_grad = refs
    rows = CAP * SUB
    for i, grad in enumerate((out_grad, in_grad)):
        part = slice(i * rows, (i + 1) * rows)
        grad[...] = sum(m[part, :].astype(jnp.float32) for m in moved).astype(grad.dtype)


def near_sum_kernel(parts, out, held, total, in_sems, out_sems):
    reads = [
        pltpu.make_async_copy(parts.at[:, far], held.at[:, far], in_sems.at[far])
        for far in range(FAR)
    ]
    writes = [
        pltpu.make_async_copy(total.at[far], out.at[far], out_sems.at[far]) for far in range(FAR)
    ]
    for read in reads:
        read.start()
    for far in range(FAR):
        reads[far].wait()
        both = sum(held[near, far].astype(jnp.float32) for near in range(NEAR))
        total[far] = both.astype(total.dtype)
        writes[far].start()
    for write in writes:
        write.wait()


def far_sum_kernel(parts, y, dx):
    total = sum(parts[far].astype(jnp.float32) for far in range(FAR)).astype(y.dtype)
    y[...] = total[:, :T]
    dx[...] = total[:, T:]


SMEM = pl.BlockSpec(memory_space=pltpu.SMEM)
VMEM = pl.BlockSpec(memory_space=pltpu.VMEM)
LIMIT = pltpu.CompilerParams(vmem_limit_bytes=24 * 1024 * 1024)
INTERPRET = False


def call(kernel, scalars, arrays, outs, scratch=()):
    bf = jnp.bfloat16
    return pl.pallas_call(
        kernel,
        out_shape=tuple(jax.ShapeDtypeStruct(dims, bf) for dims in outs),
        in_specs=[SMEM] * len(scalars) + [VMEM] * len(arrays),
        out_specs=[VMEM] * len(outs),
        scratch_shapes=[pltpu.VMEM(*dims) for dims in scratch],
        compiler_params=LIMIT,
        interpret=INTERPRET,
    )(*scalars, *arrays)


def partials_call(where, in_l, out_l, xg_parts, w_in, w_out):
    bf, f32 = jnp.bfloat16, jnp.float32
    groups = (NEAR, FAR, OWN, 2 * T)
    return pl.pallas_call(
        partials_kernel,
        out_shape=(*[jax.ShapeDtypeStruct(UNITS, bf)] * 2, pltpu.HBM(groups, bf)),
        in_specs=[SMEM] * 3 + [VMEM] * 3,
        out_specs=(VMEM, VMEM, pl.BlockSpec(memory_space=pltpu.HBM)),
        scratch_shapes=[
            pltpu.VMEM((FEAT, 2 * T), bf),
            *[pltpu.VMEM(UNITS, f32)] * 2,
            *[pltpu.VMEM((FEAT, T), f32)] * 2,
            pltpu.SemaphoreType.DMA((NEAR,)),
        ],
        compiler_params=LIMIT,
        interpret=INTERPRET,
    )(where, in_l, out_l, xg_parts, w_in, w_out)


def grads_call(where, in_l, out_l, xg_parts, act, dh):
    scratch = (((FEAT, 2 * T), jnp.bfloat16),)
    outs = ((Z,) + STEP,) * 2
    return call(grads_kernel, (where, in_l, out_l), (xg_parts, act, dh), outs, scratch)


def near_sum_call(parts):
    bf = parts.dtype
    anywhere = pl.BlockSpec(memory_space=pl.ANY)
    return pl.pallas_call(
        near_sum_kernel,
        out_shape=pltpu.HBM(parts.shape[1:], bf),
        in_specs=[anywhere],
        out_specs=pl.BlockSpec(memory_space=pltpu.HBM),
        scratch_shapes=[
            pltpu.VMEM(parts.shape, bf),
            pltpu.VMEM(parts.shape[1:], bf),
            *[pltpu.SemaphoreType.DMA((FAR,))] * 2,
        ],
        compiler_params=LIMIT,
        interpret=INTERPRET,
    )(parts)


def exchange(x, groups):
    return lax.all_to_all(
        x, ("c", "x", "y"), split_axis=0, concat_axis=0, axis_index_groups=groups
    )


def spread(x, groups):
    return exchange(jnp.broadcast_to(x[None], (len(groups[0]),) + x.shape), groups)


def neighbour(z, c):
    return ((z - c) % Z ^ 1) + c


def body(tokens, cotangent, in_blocks, in_lists, out_blocks, out_lists):
    in_l, out_l = in_lists.T, out_lists.T
    own = jnp.concatenate([tokens.T, cotangent.T], axis=1)
    where = jnp.stack([lax.axis_index("c"), lax.axis_index("z")]).astype(jnp.int32)
    own, where = lax.optimization_barrier((own, where))
    xg = spread(spread(own, FAR_GROUPS), NEAR_GROUPS)
    act, dh, parts = partials_call(where, in_l, out_l, xg, in_blocks, out_blocks)
    parts = exchange(parts, NEAR_GROUPS)
    keep, send = grads_call(where, in_l, out_l, xg, act, dh)
    got = lax.ppermute(send, "c", [(0, 1), (1, 0)])
    near, far = call(cores_kernel, (), (keep, got), ((HALF,) + STEP,) * 2)
    pairs = [
        (z * C + c, neighbour(z, c) % Z * C + c) for z in range(Z) for c in range(C)
    ]
    got = lax.ppermute(far, ("z", "c"), pairs)
    parts, got = lax.optimization_barrier((parts, got))
    own, *steps = call(pairs_kernel, (), (near, got), (STEP,) * HALF)
    moved = [
        lax.ppermute(steps[k - 1], "z", [(z, (z + 2 * k) % Z) for z in range(Z)])
        for k in (2, 1, 3)
    ]
    parts = exchange(near_sum_call(parts), FAR_GROUPS)
    y, dx = call(far_sum_kernel, (), (parts,), ((OWN, T),) * 2)
    grads = call(last_kernel, (), (own, *moved), ((CAP * SUB, BLK),) * 2)
    out_grad, in_grad = (grad.reshape(CAP, SUB, BLK) for grad in grads)
    return y.T, dx.T, in_grad, out_grad


def solution(mesh):
    fine = Mesh(mesh.devices.reshape(Z, C, X, Y), ("z", "c", "x", "y"))
    dp, mp = ("z", "c"), ("x", "y")
    blocks, lists = P(mp, None, None), P(mp, None)
    return jax.shard_map(
        body,
        mesh=fine,
        in_specs=(P(dp, mp), P(dp, mp), blocks, lists, blocks, lists),
        out_specs=(P(dp, mp), P(dp, mp), P(mp, dp, None), P(mp, dp, None)),
        check_vma=False,
    )
```

```python
import math

import jax
import jax.numpy as jnp
from jax import lax
from jax.experimental import pallas as pl
from jax.experimental.pallas import tpu as pltpu
from jax.sharding import Mesh
from jax.sharding import PartitionSpec as P

Z, C, X, Y = 8, 2, 4, 8
BLK = 128
CAP = 32
ROWS = 5
COLS = 20
T = 256
FEAT = COLS * BLK
OWN = FEAT // (X * Y)
SUB = BLK // (Z * C)
NEAR = 4
FAR = X * Y // NEAR
HALF = Z // 2
UNITS = (ROWS, BLK, T)
STEP = (2 * CAP * SUB, BLK)

ROOT_COEFF = math.sqrt(2.0 / math.pi)
CUBIC_COEFF = 0.044715


def owner_at(core, near, far):
    x = lax.rem(2 * (far // (Y // 2)) + near // 2 + core, X)
    y = lax.rem(2 * (far % (Y // 2)) + near % 2 + core, Y)
    return x * Y + y


def device_at(core, near, far):
    x = (2 * (far // (Y // 2)) + near // 2 + core) % X
    y = (2 * (far % (Y // 2)) + near % 2 + core) % Y
    return (core * X + x) * Y + y


NEAR_GROUPS = [[device_at(c, n, f) for n in range(NEAR)] for c in range(C) for f in range(FAR)]
FAR_GROUPS = [[device_at(c, n, f) for f in range(FAR)] for c in range(C) for n in range(NEAR)]


def slot_of(z, target):
    odd = lax.rem(target + Z - z, 2)
    base = z + odd * (1 - 2 * lax.rem(z, 2))
    return odd * HALF + lax.rem(target + Z - base, Z) // 2


def gelu_pair(pre):
    tanh_val = jnp.tanh(ROOT_COEFF * (pre + CUBIC_COEFF * pre * pre * pre))
    values = 0.5 * pre * (1.0 + tanh_val)
    slopes = 0.5 * (1.0 + tanh_val) + 0.5 * pre * (1.0 - tanh_val * tanh_val) * ROOT_COEFF * (
        1.0 + 3.0 * CUBIC_COEFF * pre * pre
    )
    return values, slopes


def dot(a, b, dims):
    return lax.dot_general(a, b, (dims, ((), ())), preferred_element_type=jnp.float32)


def place(lists, s):
    row, col = lists[0, s], lists[1, s]
    live = jnp.where(row >= 0, 1.0, 0.0).astype(jnp.float32)
    row = jnp.maximum(row, 0)
    return row, pl.multiple_of(jnp.maximum(col, 0) * BLK, BLK), live


def features(core, near, far):
    return pl.ds(pl.multiple_of(owner_at(core, near, far) * OWN, OWN), OWN)


def gather_features(core, parts, xg):
    for near in range(NEAR):
        for far in range(FAR):
            xg[features(core, near, far), :] = parts[near, far]


def partials_kernel(
    where, in_l, out_l, xg_parts, w_in, w_out, act, dh, parts, xg, hidden, d_act, y, dx, sems
):
    core = where[0]
    gather_features(core, xg_parts, xg)
    for total in (hidden, d_act, y, dx):
        total[...] = jnp.zeros_like(total)

    def up(s, carry):
        row, col, live = place(in_l, s)
        hidden[row] += dot(w_in[s], xg[pl.ds(col, BLK), :T], ((1,), (0,))) * live
        row, col, live = place(out_l, s)
        d_act[row] += dot(w_out[s], xg[pl.ds(col, BLK), T:], ((1,), (0,))) * live
        return carry

    def down(s, carry):
        row, col, live = place(out_l, s)
        y[pl.ds(col, BLK), :] += dot(w_out[s], act[row], ((0,), (0,))) * live
        row, col, live = place(in_l, s)
        dx[pl.ds(col, BLK), :] += dot(w_in[s], dh[row], ((0,), (0,))) * live
        return carry

    lax.fori_loop(0, CAP, up, 0, unroll=CAP)
    for row in range(ROWS):
        values, slopes = gelu_pair(hidden[row])
        act[row] = values.astype(act.dtype)
        dh[row] = (d_act[row] * slopes).astype(dh.dtype)
    lax.fori_loop(0, CAP, down, 0, unroll=CAP)
    stage = xg.reshape(NEAR, FAR, OWN, 2 * T)
    copies = []
    for near in range(NEAR):
        for far in range(FAR):
            rows = features(core, near, far)
            stage[near, far, :, :T] = y[rows, :].astype(stage.dtype)
            stage[near, far, :, T:] = dx[rows, :].astype(stage.dtype)
        copies.append(pltpu.make_async_copy(stage.at[near], parts.at[near], sems.at[near]))
        copies[-1].start()
    for copy in copies:
        copy.wait()


def grads_kernel(where, in_l, out_l, xg_parts, act, dh, keep, send, xg):
    core, z = where[0], where[1]
    gather_features(core, xg_parts, xg)
    first = core == 0
    scale = float(T * Z * C) ** -0.5
    slots = [
        [slot_of(lax.rem(z + Z - c, Z), lax.rem(target + Z - c, Z)) for target in range(Z)]
        for c in (core, 1 - core)
    ]

    def pair(p, carry):
        for which, (lists, units, lo) in enumerate(((out_l, act, T), (in_l, dh, 0))):
            two = []
            for i in range(2):
                row, col, live = place(lists, 2 * p + i)
                part = dot(units[row], xg[pl.ds(col, BLK), lo : lo + T], ((1,), (1,)))
                two.append((part * (live * scale)).reshape(Z, C, SUB, BLK))
            both = jnp.stack(two, axis=2).reshape(Z, C, 2 * SUB, BLK)
            at = pl.multiple_of((which * CAP + 2 * p) * SUB, 2 * SUB)
            mine = jnp.where(first, both[:, 0], both[:, 1]).astype(keep.dtype)
            others = jnp.where(first, both[:, 1], both[:, 0]).astype(send.dtype)
            for target in range(Z):
                keep[slots[0][target], pl.ds(at, 2 * SUB), :] = mine[target]
                send[slots[1][target], pl.ds(at, 2 * SUB), :] = others[target]
        return carry

    lax.fori_loop(0, CAP // 2, pair, 0, unroll=CAP // 2)


def cores_kernel(keep, got, near, far):
    for slot in range(Z):
        both = keep[slot].astype(jnp.float32) + got[slot].astype(jnp.float32)
        out = near if slot < HALF else far
        out[slot % HALF] = both.astype(out.dtype)


def pairs_kernel(near, got, *outs):
    for slot, out in enumerate(outs):
        both = near[slot].astype(jnp.float32) + got[slot].astype(jnp.float32)
        out[...] = both.astype(out.dtype)


def near_sum_kernel(parts, out, held, total, in_sems, out_sems):
    reads = [
        pltpu.make_async_copy(parts.at[:, far], held.at[:, far], in_sems.at[far])
        for far in range(FAR)
    ]
    writes = [
        pltpu.make_async_copy(total.at[far], out.at[far], out_sems.at[far]) for far in range(FAR)
    ]
    for read in reads:
        read.start()
    for far in range(FAR):
        reads[far].wait()
        both = sum(held[near, far].astype(jnp.float32) for near in range(NEAR))
        total[far] = both.astype(total.dtype)
        writes[far].start()
    for write in writes:
        write.wait()


def last_kernel(parts, *refs):
    *moved, y, dx, out_grad, in_grad = refs
    total = sum(parts[far].astype(jnp.float32) for far in range(FAR)).astype(y.dtype)
    y[...] = total[:, :T]
    dx[...] = total[:, T:]
    rows = CAP * SUB
    for i, grad in enumerate((out_grad, in_grad)):
        part = slice(i * rows, (i + 1) * rows)
        grad[...] = sum(m[part, :].astype(jnp.float32) for m in moved).astype(grad.dtype)


SMEM = pl.BlockSpec(memory_space=pltpu.SMEM)
VMEM = pl.BlockSpec(memory_space=pltpu.VMEM)
LIMIT = pltpu.CompilerParams(vmem_limit_bytes=24 * 1024 * 1024)
INTERPRET = False


def call(kernel, scalars, arrays, outs, scratch=()):
    bf = jnp.bfloat16
    return pl.pallas_call(
        kernel,
        out_shape=tuple(jax.ShapeDtypeStruct(dims, bf) for dims in outs),
        in_specs=[SMEM] * len(scalars) + [VMEM] * len(arrays),
        out_specs=[VMEM] * len(outs),
        scratch_shapes=[pltpu.VMEM(*dims) for dims in scratch],
        compiler_params=LIMIT,
        interpret=INTERPRET,
    )(*scalars, *arrays)


def partials_call(where, in_l, out_l, xg_parts, w_in, w_out):
    bf, f32 = jnp.bfloat16, jnp.float32
    groups = (NEAR, FAR, OWN, 2 * T)
    return pl.pallas_call(
        partials_kernel,
        out_shape=(*[jax.ShapeDtypeStruct(UNITS, bf)] * 2, pltpu.HBM(groups, bf)),
        in_specs=[SMEM] * 3 + [VMEM] * 3,
        out_specs=(VMEM, VMEM, pl.BlockSpec(memory_space=pltpu.HBM)),
        scratch_shapes=[
            pltpu.VMEM((FEAT, 2 * T), bf),
            *[pltpu.VMEM(UNITS, f32)] * 2,
            *[pltpu.VMEM((FEAT, T), f32)] * 2,
            pltpu.SemaphoreType.DMA((NEAR,)),
        ],
        compiler_params=LIMIT,
        interpret=INTERPRET,
    )(where, in_l, out_l, xg_parts, w_in, w_out)


def grads_call(where, in_l, out_l, xg_parts, act, dh):
    scratch = (((FEAT, 2 * T), jnp.bfloat16),)
    outs = ((Z,) + STEP,) * 2
    return call(grads_kernel, (where, in_l, out_l), (xg_parts, act, dh), outs, scratch)


def near_sum_call(parts):
    bf = parts.dtype
    anywhere = pl.BlockSpec(memory_space=pl.ANY)
    return pl.pallas_call(
        near_sum_kernel,
        out_shape=pltpu.HBM(parts.shape[1:], bf),
        in_specs=[anywhere],
        out_specs=pl.BlockSpec(memory_space=pltpu.HBM),
        scratch_shapes=[
            pltpu.VMEM(parts.shape, bf),
            pltpu.VMEM(parts.shape[1:], bf),
            *[pltpu.SemaphoreType.DMA((FAR,))] * 2,
        ],
        compiler_params=LIMIT,
        interpret=INTERPRET,
    )(parts)


def exchange(x, groups):
    return lax.all_to_all(
        x, ("c", "x", "y"), split_axis=0, concat_axis=0, axis_index_groups=groups
    )


def spread(x, groups):
    return exchange(jnp.broadcast_to(x[None], (len(groups[0]),) + x.shape), groups)


def neighbour(z, c):
    return ((z - c) % Z ^ 1) + c


def body(tokens, cotangent, in_blocks, in_lists, out_blocks, out_lists):
    in_l, out_l = in_lists.T, out_lists.T
    own = jnp.concatenate([tokens.T, cotangent.T], axis=1)
    where = jnp.stack([lax.axis_index("c"), lax.axis_index("z")]).astype(jnp.int32)
    own, where = lax.optimization_barrier((own, where))
    xg = spread(spread(own, FAR_GROUPS), NEAR_GROUPS)
    act, dh, parts = partials_call(where, in_l, out_l, xg, in_blocks, out_blocks)
    parts = exchange(parts, NEAR_GROUPS)
    keep, send = grads_call(where, in_l, out_l, xg, act, dh)
    got = lax.ppermute(send, "c", [(0, 1), (1, 0)])
    near, far = call(cores_kernel, (), (keep, got), ((HALF,) + STEP,) * 2)
    pairs = [
        (z * C + c, neighbour(z, c) % Z * C + c) for z in range(Z) for c in range(C)
    ]
    got = lax.ppermute(far, ("z", "c"), pairs)
    parts, got = lax.optimization_barrier((parts, got))
    own, *steps = call(pairs_kernel, (), (near, got), (STEP,) * HALF)
    moved = [
        lax.ppermute(steps[k - 1], "z", [(z, (z + 2 * k) % Z) for z in range(Z)])
        for k in (2, 1, 3)
    ]
    parts = exchange(near_sum_call(parts), FAR_GROUPS)
    outs = ((OWN, T),) * 2 + ((CAP * SUB, BLK),) * 2
    y, dx, *grads = call(last_kernel, (), (parts, own, *moved), outs)
    out_grad, in_grad = (grad.reshape(CAP, SUB, BLK) for grad in grads)
    return y.T, dx.T, in_grad, out_grad


def solution(mesh):
    fine = Mesh(mesh.devices.reshape(Z, C, X, Y), ("z", "c", "x", "y"))
    dp, mp = ("z", "c"), ("x", "y")
    blocks, lists = P(mp, None, None), P(mp, None)
    return jax.shard_map(
        body,
        mesh=fine,
        in_specs=(P(dp, mp), P(dp, mp), blocks, lists, blocks, lists),
        out_specs=(P(dp, mp), P(dp, mp), P(mp, dp, None), P(mp, dp, None)),
        check_vma=False,
    )
```

```python
import math

import jax
import jax.numpy as jnp
from jax import lax
from jax.experimental import pallas as pl
from jax.experimental.pallas import tpu as pltpu
from jax.sharding import Mesh
from jax.sharding import PartitionSpec as P

Z, C, X, Y = 8, 2, 4, 8
BLK = 128
CAP = 32
ROWS = 5
COLS = 20
T = 256
FEAT = COLS * BLK
OWN = FEAT // (X * Y)
SUB = BLK // (Z * C)
NEAR = 4
FAR = X * Y // NEAR
HALF = Z // 2
UNITS = (ROWS, BLK, T)
STEP = (2 * CAP * SUB, BLK)

ROOT_COEFF = math.sqrt(2.0 / math.pi)
CUBIC_COEFF = 0.044715


def owner_at(core, near, far):
    x = lax.rem(2 * (far // (Y // 2)) + near // 2 + core, X)
    y = lax.rem(2 * (far % (Y // 2)) + near % 2 + core, Y)
    return x * Y + y


def device_at(core, near, far):
    x = (2 * (far // (Y // 2)) + near // 2 + core) % X
    y = (2 * (far % (Y // 2)) + near % 2 + core) % Y
    return (core * X + x) * Y + y


NEAR_GROUPS = [[device_at(c, n, f) for n in range(NEAR)] for c in range(C) for f in range(FAR)]
FAR_GROUPS = [[device_at(c, n, f) for f in range(FAR)] for c in range(C) for n in range(NEAR)]


def slot_of(z, target):
    odd = lax.rem(target + Z - z, 2)
    base = z + odd * (1 - 2 * lax.rem(z, 2))
    return odd * HALF + lax.rem(target + Z - base, Z) // 2


def gelu_pair(pre):
    tanh_val = jnp.tanh(ROOT_COEFF * (pre + CUBIC_COEFF * pre * pre * pre))
    values = 0.5 * pre * (1.0 + tanh_val)
    slopes = 0.5 * (1.0 + tanh_val) + 0.5 * pre * (1.0 - tanh_val * tanh_val) * ROOT_COEFF * (
        1.0 + 3.0 * CUBIC_COEFF * pre * pre
    )
    return values, slopes


def dot(a, b, dims):
    return lax.dot_general(a, b, (dims, ((), ())), preferred_element_type=jnp.float32)


def place(lists, s):
    row, col = lists[0, s], lists[1, s]
    live = jnp.where(row >= 0, 1.0, 0.0).astype(jnp.float32)
    row = jnp.maximum(row, 0)
    return row, pl.multiple_of(jnp.maximum(col, 0) * BLK, BLK), live


def features(core, near, far):
    return pl.ds(pl.multiple_of(owner_at(core, near, far) * OWN, OWN), OWN)


def gather_features(core, parts, xg):
    for near in range(NEAR):
        for far in range(FAR):
            xg[features(core, near, far), :] = parts[near, far]


def partials_kernel(
    where, in_l, out_l, xg_parts, w_in, w_out, act, dh, parts, xg, hidden, d_act, y, dx, sems
):
    core = where[0]
    gather_features(core, xg_parts, xg)
    for total in (hidden, d_act, y, dx):
        total[...] = jnp.zeros_like(total)

    def up(s, carry):
        row, col, live = place(in_l, s)
        hidden[row] += dot(w_in[s], xg[pl.ds(col, BLK), :T], ((1,), (0,))) * live
        row, col, live = place(out_l, s)
        d_act[row] += dot(w_out[s], xg[pl.ds(col, BLK), T:], ((1,), (0,))) * live
        return carry

    def down(s, carry):
        row, col, live = place(out_l, s)
        y[pl.ds(col, BLK), :] += dot(w_out[s], act[row], ((0,), (0,))) * live
        row, col, live = place(in_l, s)
        dx[pl.ds(col, BLK), :] += dot(w_in[s], dh[row], ((0,), (0,))) * live
        return carry

    lax.fori_loop(0, CAP, up, 0, unroll=CAP)
    for row in range(ROWS):
        values, slopes = gelu_pair(hidden[row])
        act[row] = values.astype(act.dtype)
        dh[row] = (d_act[row] * slopes).astype(dh.dtype)
    lax.fori_loop(0, CAP, down, 0, unroll=CAP)
    stage = xg.reshape(NEAR, FAR, OWN, 2 * T)
    copies = []
    for near in range(NEAR):
        for far in range(FAR):
            rows = features(core, near, far)
            stage[near, far, :, :T] = y[rows, :].astype(stage.dtype)
            stage[near, far, :, T:] = dx[rows, :].astype(stage.dtype)
        copies.append(pltpu.make_async_copy(stage.at[near], parts.at[near], sems.at[near]))
        copies[-1].start()
    for copy in copies:
        copy.wait()


def grads_kernel(where, in_l, out_l, xg_parts, act, dh, keep, send, xg):
    core, z = where[0], where[1]
    gather_features(core, xg_parts, xg)
    first = core == 0
    scale = float(T * Z * C) ** -0.5
    slots = [
        [slot_of(lax.rem(z + Z - c, Z), lax.rem(target + Z - c, Z)) for target in range(Z)]
        for c in (core, 1 - core)
    ]

    def pair(p, carry):
        for which, (lists, units, lo) in enumerate(((out_l, act, T), (in_l, dh, 0))):
            two = []
            for i in range(2):
                row, col, live = place(lists, 2 * p + i)
                part = dot(units[row], xg[pl.ds(col, BLK), lo : lo + T], ((1,), (1,)))
                two.append((part * (live * scale)).reshape(Z, C, SUB, BLK))
            both = jnp.stack(two, axis=2).reshape(Z, C, 2 * SUB, BLK)
            at = pl.multiple_of((which * CAP + 2 * p) * SUB, 2 * SUB)
            mine = jnp.where(first, both[:, 0], both[:, 1]).astype(keep.dtype)
            others = jnp.where(first, both[:, 1], both[:, 0]).astype(send.dtype)
            for target in range(Z):
                keep[slots[0][target], pl.ds(at, 2 * SUB), :] = mine[target]
                send[slots[1][target], pl.ds(at, 2 * SUB), :] = others[target]
        return carry

    lax.fori_loop(0, CAP // 2, pair, 0, unroll=CAP // 2)


def cores_kernel(keep, got, near, far):
    for slot in range(Z):
        both = keep[slot].astype(jnp.float32) + got[slot].astype(jnp.float32)
        out = near if slot < HALF else far
        out[slot % HALF] = both.astype(out.dtype)


def pairs_kernel(near, got, *outs):
    for slot, out in enumerate(outs):
        both = near[slot].astype(jnp.float32) + got[slot].astype(jnp.float32)
        out[...] = both.astype(out.dtype)


def near_sum_kernel(parts, out, held, total, in_sems, out_sems):
    reads = [
        pltpu.make_async_copy(parts.at[:, far], held.at[:, far], in_sems.at[far])
        for far in range(FAR)
    ]
    writes = [
        pltpu.make_async_copy(total.at[far], out.at[far], out_sems.at[far]) for far in range(FAR)
    ]
    for read in reads:
        read.start()
    for far in range(FAR):
        reads[far].wait()
        both = sum(held[near, far].astype(jnp.float32) for near in range(NEAR))
        total[far] = both.astype(total.dtype)
        writes[far].start()
    for write in writes:
        write.wait()


def last_kernel(parts, *refs):
    *moved, y, dx, out_grad, in_grad = refs
    total = sum(parts[far].astype(jnp.float32) for far in range(FAR)).astype(y.dtype)
    y[...] = total[:, :T]
    dx[...] = total[:, T:]
    rows = CAP * SUB
    for i, grad in enumerate((out_grad, in_grad)):
        part = slice(i * rows, (i + 1) * rows)
        grad[...] = sum(m[part, :].astype(jnp.float32) for m in moved).astype(grad.dtype)


SMEM = pl.BlockSpec(memory_space=pltpu.SMEM)
VMEM = pl.BlockSpec(memory_space=pltpu.VMEM)
LIMIT = pltpu.CompilerParams(vmem_limit_bytes=24 * 1024 * 1024)
INTERPRET = False


def call(kernel, scalars, arrays, outs, scratch=()):
    bf = jnp.bfloat16
    return pl.pallas_call(
        kernel,
        out_shape=tuple(jax.ShapeDtypeStruct(dims, bf) for dims in outs),
        in_specs=[SMEM] * len(scalars) + [VMEM] * len(arrays),
        out_specs=[VMEM] * len(outs),
        scratch_shapes=[pltpu.VMEM(*dims) for dims in scratch],
        compiler_params=LIMIT,
        interpret=INTERPRET,
    )(*scalars, *arrays)


def partials_call(where, in_l, out_l, xg_parts, w_in, w_out):
    bf, f32 = jnp.bfloat16, jnp.float32
    groups = (NEAR, FAR, OWN, 2 * T)
    return pl.pallas_call(
        partials_kernel,
        out_shape=(*[jax.ShapeDtypeStruct(UNITS, bf)] * 2, pltpu.HBM(groups, bf)),
        in_specs=[SMEM] * 3 + [VMEM] * 3,
        out_specs=(VMEM, VMEM, pl.BlockSpec(memory_space=pltpu.HBM)),
        scratch_shapes=[
            pltpu.VMEM((FEAT, 2 * T), bf),
            *[pltpu.VMEM(UNITS, f32)] * 2,
            *[pltpu.VMEM((FEAT, T), f32)] * 2,
            pltpu.SemaphoreType.DMA((NEAR,)),
        ],
        compiler_params=LIMIT,
        interpret=INTERPRET,
    )(where, in_l, out_l, xg_parts, w_in, w_out)


def grads_call(where, in_l, out_l, xg_parts, act, dh):
    scratch = (((FEAT, 2 * T), jnp.bfloat16),)
    outs = ((Z,) + STEP,) * 2
    return call(grads_kernel, (where, in_l, out_l), (xg_parts, act, dh), outs, scratch)


def near_sum_call(parts):
    bf = parts.dtype
    anywhere = pl.BlockSpec(memory_space=pl.ANY)
    return pl.pallas_call(
        near_sum_kernel,
        out_shape=pltpu.HBM(parts.shape[1:], bf),
        in_specs=[anywhere],
        out_specs=pl.BlockSpec(memory_space=pltpu.HBM),
        scratch_shapes=[
            pltpu.VMEM(parts.shape, bf),
            pltpu.VMEM(parts.shape[1:], bf),
            *[pltpu.SemaphoreType.DMA((FAR,))] * 2,
        ],
        compiler_params=LIMIT,
        interpret=INTERPRET,
    )(parts)


def exchange(x, groups):
    return lax.all_to_all(
        x, ("c", "x", "y"), split_axis=0, concat_axis=0, axis_index_groups=groups
    )


def spread(x, groups):
    return exchange(jnp.broadcast_to(x[None], (len(groups[0]),) + x.shape), groups)


def neighbour(z, c):
    return ((z - c) % Z ^ 1) + c


def body(tokens, cotangent, in_blocks, in_lists, out_blocks, out_lists):
    in_l, out_l = in_lists.T, out_lists.T
    own = jnp.concatenate([tokens.T, cotangent.T], axis=1)
    where = jnp.stack([lax.axis_index("c"), lax.axis_index("z")]).astype(jnp.int32)
    own, where = lax.optimization_barrier((own, where))
    xg = spread(spread(own, FAR_GROUPS), NEAR_GROUPS)
    act, dh, parts = partials_call(where, in_l, out_l, xg, in_blocks, out_blocks)
    parts = exchange(parts, NEAR_GROUPS)
    keep, send = grads_call(where, in_l, out_l, xg, act, dh)
    got = lax.ppermute(send, "c", [(0, 1), (1, 0)])
    near, far = call(cores_kernel, (), (keep, got), ((HALF,) + STEP,) * 2)
    pairs = [
        (z * C + c, neighbour(z, c) % Z * C + c) for z in range(Z) for c in range(C)
    ]
    got = lax.ppermute(far, ("z", "c"), pairs)
    parts, got = lax.optimization_barrier((parts, got))
    own, *steps = call(pairs_kernel, (), (near, got), (STEP,) * HALF)
    moved = [
        lax.ppermute(steps[k - 1], "z", [(z, (z + 2 * k) % Z) for z in range(Z)])
        for k in (1, 3, 2)
    ]
    parts = exchange(near_sum_call(parts), FAR_GROUPS)
    outs = ((OWN, T),) * 2 + ((CAP * SUB, BLK),) * 2
    y, dx, *grads = call(last_kernel, (), (parts, own, *moved), outs)
    out_grad, in_grad = (grad.reshape(CAP, SUB, BLK) for grad in grads)
    return y.T, dx.T, in_grad, out_grad


def solution(mesh):
    fine = Mesh(mesh.devices.reshape(Z, C, X, Y), ("z", "c", "x", "y"))
    dp, mp = ("z", "c"), ("x", "y")
    blocks, lists = P(mp, None, None), P(mp, None)
    return jax.shard_map(
        body,
        mesh=fine,
        in_specs=(P(dp, mp), P(dp, mp), blocks, lists, blocks, lists),
        out_specs=(P(dp, mp), P(dp, mp), P(mp, dp, None), P(mp, dp, None)),
        check_vma=False,
    )
```

```python
import math

import jax
import jax.numpy as jnp
from jax import lax
from jax.experimental import pallas as pl
from jax.experimental.pallas import tpu as pltpu
from jax.sharding import Mesh
from jax.sharding import PartitionSpec as P

Z, C, X, Y = 8, 2, 4, 8
BLK = 128
CAP = 32
ROWS = 5
COLS = 20
T = 256
FEAT = COLS * BLK
OWN = FEAT // (X * Y)
SUB = BLK // (Z * C)
NEAR = 4
FAR = X * Y // NEAR
HALF = Z // 2
UNITS = (ROWS, BLK, T)
STEP = (2 * CAP * SUB, BLK)

ROOT_COEFF = math.sqrt(2.0 / math.pi)
CUBIC_COEFF = 0.044715


def owner_at(core, near, far):
    x = lax.rem(2 * (far // (Y // 2)) + near // 2 + core, X)
    y = lax.rem(2 * (far % (Y // 2)) + near % 2 + core, Y)
    return x * Y + y


def device_at(core, near, far):
    x = (2 * (far // (Y // 2)) + near // 2 + core) % X
    y = (2 * (far % (Y // 2)) + near % 2 + core) % Y
    return (core * X + x) * Y + y


NEAR_GROUPS = [[device_at(c, n, f) for n in range(NEAR)] for c in range(C) for f in range(FAR)]
FAR_GROUPS = [[device_at(c, n, f) for f in range(FAR)] for c in range(C) for n in range(NEAR)]


def slot_of(z, target):
    odd = lax.rem(target + Z - z, 2)
    base = z + odd * (1 - 2 * lax.rem(z, 2))
    return odd * HALF + lax.rem(target + Z - base, Z) // 2


def gelu_pair(pre):
    tanh_val = jnp.tanh(ROOT_COEFF * (pre + CUBIC_COEFF * pre * pre * pre))
    values = 0.5 * pre * (1.0 + tanh_val)
    slopes = 0.5 * (1.0 + tanh_val) + 0.5 * pre * (1.0 - tanh_val * tanh_val) * ROOT_COEFF * (
        1.0 + 3.0 * CUBIC_COEFF * pre * pre
    )
    return values, slopes


def dot(a, b, dims):
    return lax.dot_general(a, b, (dims, ((), ())), preferred_element_type=jnp.float32)


def place(lists, s):
    row, col = lists[0, s], lists[1, s]
    live = jnp.where(row >= 0, 1.0, 0.0).astype(jnp.float32)
    row = jnp.maximum(row, 0)
    return row, pl.multiple_of(jnp.maximum(col, 0) * BLK, BLK), live


def features(core, near, far):
    return pl.ds(pl.multiple_of(owner_at(core, near, far) * OWN, OWN), OWN)


def gather_features(core, parts, xg):
    for near in range(NEAR):
        for far in range(FAR):
            xg[features(core, near, far), :] = parts[near, far]


def partials_kernel(
    where, in_l, out_l, xg_parts, w_in, w_out, act, dh, parts, xg, hidden, d_act, y, dx, sems
):
    core = where[0]
    gather_features(core, xg_parts, xg)
    for total in (hidden, d_act, y, dx):
        total[...] = jnp.zeros_like(total)

    def up(s, carry):
        row, col, live = place(in_l, s)
        hidden[row] += dot(w_in[s], xg[pl.ds(col, BLK), :T], ((1,), (0,))) * live
        row, col, live = place(out_l, s)
        d_act[row] += dot(w_out[s], xg[pl.ds(col, BLK), T:], ((1,), (0,))) * live
        return carry

    def down(lists, weights, units, total):
        def product(s, carry):
            row, col, live = place(lists, s)
            total[pl.ds(col, BLK), :] += dot(weights[s], units[row], ((0,), (0,))) * live
            return carry

        lax.fori_loop(0, CAP, product, 0, unroll=CAP)

    lax.fori_loop(0, CAP, up, 0, unroll=CAP)
    for row in range(ROWS):
        values, slopes = gelu_pair(hidden[row])
        act[row] = values.astype(act.dtype)
        dh[row] = (d_act[row] * slopes).astype(dh.dtype)
    stage = xg.reshape(NEAR, FAR, OWN, 2 * T)
    copies = []
    for half, (lists, weights, units, total) in enumerate(
        ((out_l, w_out, act, y), (in_l, w_in, dh, dx))
    ):
        down(lists, weights, units, total)
        cols = pl.ds(half * T, T)
        for near in range(NEAR):
            for far in range(FAR):
                rows = features(core, near, far)
                stage[near, far, :, cols] = total[rows, :].astype(stage.dtype)
            source, target = stage.at[near, :, :, cols], parts.at[near, :, :, cols]
            copies.append(pltpu.make_async_copy(source, target, sems.at[half, near]))
            copies[-1].start()
    for copy in copies:
        copy.wait()


def grads_kernel(where, in_l, out_l, xg_parts, act, dh, keep, send, xg):
    core, z = where[0], where[1]
    gather_features(core, xg_parts, xg)
    first = core == 0
    scale = float(T * Z * C) ** -0.5
    slots = [
        [slot_of(lax.rem(z + Z - c, Z), lax.rem(target + Z - c, Z)) for target in range(Z)]
        for c in (core, 1 - core)
    ]

    def pair(p, carry):
        for which, (lists, units, lo) in enumerate(((out_l, act, T), (in_l, dh, 0))):
            two = []
            for i in range(2):
                row, col, live = place(lists, 2 * p + i)
                part = dot(units[row], xg[pl.ds(col, BLK), lo : lo + T], ((1,), (1,)))
                two.append((part * (live * scale)).reshape(Z, C, SUB, BLK))
            both = jnp.stack(two, axis=2).reshape(Z, C, 2 * SUB, BLK)
            at = pl.multiple_of((which * CAP + 2 * p) * SUB, 2 * SUB)
            mine = jnp.where(first, both[:, 0], both[:, 1]).astype(keep.dtype)
            others = jnp.where(first, both[:, 1], both[:, 0]).astype(send.dtype)
            for target in range(Z):
                keep[slots[0][target], pl.ds(at, 2 * SUB), :] = mine[target]
                send[slots[1][target], pl.ds(at, 2 * SUB), :] = others[target]
        return carry

    lax.fori_loop(0, CAP // 2, pair, 0, unroll=CAP // 2)


def cores_kernel(keep, got, near, far):
    for slot in range(Z):
        both = keep[slot].astype(jnp.float32) + got[slot].astype(jnp.float32)
        out = near if slot < HALF else far
        out[slot % HALF] = both.astype(out.dtype)


def pairs_kernel(near, got, *outs):
    for slot, out in enumerate(outs):
        both = near[slot].astype(jnp.float32) + got[slot].astype(jnp.float32)
        out[...] = both.astype(out.dtype)


def near_sum_kernel(parts, out, held, total, in_sems, out_sems):
    reads = [
        pltpu.make_async_copy(parts.at[:, far], held.at[:, far], in_sems.at[far])
        for far in range(FAR)
    ]
    writes = [
        pltpu.make_async_copy(total.at[far], out.at[far], out_sems.at[far]) for far in range(FAR)
    ]
    for read in reads:
        read.start()
    for far in range(FAR):
        reads[far].wait()
        both = sum(held[near, far].astype(jnp.float32) for near in range(NEAR))
        total[far] = both.astype(total.dtype)
        writes[far].start()
    for write in writes:
        write.wait()


def last_kernel(parts, *refs):
    *moved, y, dx, out_grad, in_grad = refs
    total = sum(parts[far].astype(jnp.float32) for far in range(FAR)).astype(y.dtype)
    y[...] = total[:, :T]
    dx[...] = total[:, T:]
    rows = CAP * SUB
    for i, grad in enumerate((out_grad, in_grad)):
        part = slice(i * rows, (i + 1) * rows)
        grad[...] = sum(m[part, :].astype(jnp.float32) for m in moved).astype(grad.dtype)


SMEM = pl.BlockSpec(memory_space=pltpu.SMEM)
VMEM = pl.BlockSpec(memory_space=pltpu.VMEM)
LIMIT = pltpu.CompilerParams(vmem_limit_bytes=24 * 1024 * 1024)
INTERPRET = False


def call(kernel, scalars, arrays, outs, scratch=()):
    bf = jnp.bfloat16
    return pl.pallas_call(
        kernel,
        out_shape=tuple(jax.ShapeDtypeStruct(dims, bf) for dims in outs),
        in_specs=[SMEM] * len(scalars) + [VMEM] * len(arrays),
        out_specs=[VMEM] * len(outs),
        scratch_shapes=[pltpu.VMEM(*dims) for dims in scratch],
        compiler_params=LIMIT,
        interpret=INTERPRET,
    )(*scalars, *arrays)


def partials_call(where, in_l, out_l, xg_parts, w_in, w_out):
    bf, f32 = jnp.bfloat16, jnp.float32
    groups = (NEAR, FAR, OWN, 2 * T)
    return pl.pallas_call(
        partials_kernel,
        out_shape=(*[jax.ShapeDtypeStruct(UNITS, bf)] * 2, pltpu.HBM(groups, bf)),
        in_specs=[SMEM] * 3 + [VMEM] * 3,
        out_specs=(VMEM, VMEM, pl.BlockSpec(memory_space=pltpu.HBM)),
        scratch_shapes=[
            pltpu.VMEM((FEAT, 2 * T), bf),
            *[pltpu.VMEM(UNITS, f32)] * 2,
            *[pltpu.VMEM((FEAT, T), f32)] * 2,
            pltpu.SemaphoreType.DMA((2, NEAR)),
        ],
        compiler_params=LIMIT,
        interpret=INTERPRET,
    )(where, in_l, out_l, xg_parts, w_in, w_out)


def grads_call(where, in_l, out_l, xg_parts, act, dh):
    scratch = (((FEAT, 2 * T), jnp.bfloat16),)
    outs = ((Z,) + STEP,) * 2
    return call(grads_kernel, (where, in_l, out_l), (xg_parts, act, dh), outs, scratch)


def near_sum_call(parts):
    bf = parts.dtype
    anywhere = pl.BlockSpec(memory_space=pl.ANY)
    return pl.pallas_call(
        near_sum_kernel,
        out_shape=pltpu.HBM(parts.shape[1:], bf),
        in_specs=[anywhere],
        out_specs=pl.BlockSpec(memory_space=pltpu.HBM),
        scratch_shapes=[
            pltpu.VMEM(parts.shape, bf),
            pltpu.VMEM(parts.shape[1:], bf),
            *[pltpu.SemaphoreType.DMA((FAR,))] * 2,
        ],
        compiler_params=LIMIT,
        interpret=INTERPRET,
    )(parts)


def exchange(x, groups):
    return lax.all_to_all(
        x, ("c", "x", "y"), split_axis=0, concat_axis=0, axis_index_groups=groups
    )


def spread(x, groups):
    return exchange(jnp.broadcast_to(x[None], (len(groups[0]),) + x.shape), groups)


def neighbour(z, c):
    return ((z - c) % Z ^ 1) + c


def body(tokens, cotangent, in_blocks, in_lists, out_blocks, out_lists):
    in_l, out_l = in_lists.T, out_lists.T
    own = jnp.concatenate([tokens.T, cotangent.T], axis=1)
    where = jnp.stack([lax.axis_index("c"), lax.axis_index("z")]).astype(jnp.int32)
    own, where = lax.optimization_barrier((own, where))
    xg = spread(spread(own, FAR_GROUPS), NEAR_GROUPS)
    act, dh, parts = partials_call(where, in_l, out_l, xg, in_blocks, out_blocks)
    parts = exchange(parts, NEAR_GROUPS)
    keep, send = grads_call(where, in_l, out_l, xg, act, dh)
    got = lax.ppermute(send, "c", [(0, 1), (1, 0)])
    near, far = call(cores_kernel, (), (keep, got), ((HALF,) + STEP,) * 2)
    pairs = [
        (z * C + c, neighbour(z, c) % Z * C + c) for z in range(Z) for c in range(C)
    ]
    got = lax.ppermute(far, ("z", "c"), pairs)
    parts, got = lax.optimization_barrier((parts, got))
    own, *steps = call(pairs_kernel, (), (near, got), (STEP,) * HALF)
    moved = [
        lax.ppermute(steps[k - 1], "z", [(z, (z + 2 * k) % Z) for z in range(Z)])
        for k in (2, 1, 3)
    ]
    parts = exchange(near_sum_call(parts), FAR_GROUPS)
    outs = ((OWN, T),) * 2 + ((CAP * SUB, BLK),) * 2
    y, dx, *grads = call(last_kernel, (), (parts, own, *moved), outs)
    out_grad, in_grad = (grad.reshape(CAP, SUB, BLK) for grad in grads)
    return y.T, dx.T, in_grad, out_grad


def solution(mesh):
    fine = Mesh(mesh.devices.reshape(Z, C, X, Y), ("z", "c", "x", "y"))
    dp, mp = ("z", "c"), ("x", "y")
    blocks, lists = P(mp, None, None), P(mp, None)
    return jax.shard_map(
        body,
        mesh=fine,
        in_specs=(P(dp, mp), P(dp, mp), blocks, lists, blocks, lists),
        out_specs=(P(dp, mp), P(dp, mp), P(mp, dp, None), P(mp, dp, None)),
        check_vma=False,
    )
```
